256 devices in a mesh: tr: 32 (over x, y, core), su: 8 (over z).
Axes of the slice: x: 4, y: 4, z: 8, core: 2. Of those that a mesh axis runs over, the one named last changes fastest.
Arguments:
- amplitudes: bfloat16 [16, 32, 384, 384], P(None, 'tr', 'su'), as said below
- integrals: bfloat16 [32, 384, 32, 384], P('su', None, 'tr'), as said below
- occupied_irreps: int32 [32], replicated, may hold values from 0 to 7, as said below
- virtual_irreps: int32 [384], replicated, may hold values from 0 to 7, as said below
Outputs:
- update: bfloat16 [16, 32, 384, 384], P(None, 'tr', 'su')
The draws below stay inside these ranges and needn't reach their ends.
Inputs may be any that keep to these rules, and one draw needn't show every extreme that they name: `occupied_irreps`: non-decreasing: the occupied orbitals come grouped by irrep. `virtual_irreps`: non-decreasing: the virtual orbitals come grouped by irrep. amplitudes[i, k, a, c] is 0 unless occupied_irreps[i] xor occupied_irreps[k] xor virtual_irreps[a] xor virtual_irreps[c] is 0. integrals[k, c, j, b] is 0 unless occupied_irreps[k] xor virtual_irreps[c] xor occupied_irreps[j] xor virtual_irreps[b] is 0.
All inputs are finite; a program needn't handle non-finite values.
Results may differ from the reference program's by a relative error of at most 0.001.
Values may be sent and summed in bfloat16 or wider, within the bound.
No kernel may reach another device: no remote copies, remote signals or barrier semaphores. Data moves between devices by JAX's collectives and lax.ppermute only.
A program may use at most 128 MiB of HBM per device.

```python
import jax
import jax.numpy as jnp
from jax import lax

O = 32
V = 384
IW = 16


def irrep_labels(key, count, salt):
    key = jax.random.fold_in(key, salt)
    inner = jnp.sort(jax.random.randint(key, (count - 2,), 0, 8)).astype(jnp.int32)
    return jnp.concatenate([jnp.zeros((1,), jnp.int32), inner, jnp.full((1,), 7, jnp.int32)])


def symmetric(first, second, third, fourth):
    total = jnp.bitwise_xor(first[:, None, None, None], second[None, :, None, None])
    total = jnp.bitwise_xor(total, third[None, None, :, None])
    total = jnp.bitwise_xor(total, fourth[None, None, None, :])
    return total == 0


def draw_occupied_irreps(key, part):
    return irrep_labels(key, O, 11)


def draw_virtual_irreps(key, part):
    return irrep_labels(key, V, 12)


def draw_amplitudes(key, part):
    occupied = irrep_labels(key, O, 11)
    virtual = irrep_labels(key, V, 12)
    key = jax.random.fold_in(key, 21)
    value_key = jax.random.fold_in(key, 0)
    shape = (IW, O, V, V)
    values = jnp.clip(jax.random.normal(value_key, shape, jnp.float32), -6.0, 6.0)
    keep = symmetric(occupied[:IW], occupied, virtual, virtual)
    return jnp.where(keep, values, 0.0).astype(jnp.bfloat16)


def draw_integrals(key, part):
    occupied = irrep_labels(key, O, 11)
    virtual = irrep_labels(key, V, 12)
    key = jax.random.fold_in(key, 22)
    shape = (O, V, O, V)
    factor = (8.0 / (O * V)) ** 0.5
    values = jnp.clip(jax.random.normal(key, shape, jnp.float32), -6.0, 6.0) * factor
    keep = symmetric(occupied, virtual, occupied, virtual)
    return jnp.where(keep, values, 0.0).astype(jnp.bfloat16)


def setup_inputs(seed: int = 0) -> dict:
    streams_of = jax.random.split(jax.random.key(seed), 5)
    return {
        "amplitudes": draw_amplitudes(jax.random.fold_in(streams_of[4], 71), 0),
        "integrals": draw_integrals(jax.random.fold_in(streams_of[4], 71), 0),
        "occupied_irreps": draw_occupied_irreps(jax.random.fold_in(streams_of[4], 71), 0),
        "virtual_irreps": draw_virtual_irreps(jax.random.fold_in(streams_of[4], 71), 0),
    }


def reference(amplitudes, integrals, occupied_irreps, virtual_irreps):
    matrix_w = integrals.reshape(O * V, O * V)

    def one_row(slab):
        left = jnp.transpose(slab, (1, 0, 2)).reshape(V, O * V)
        product = jnp.dot(left, matrix_w, preferred_element_type=jnp.float32)
        return jnp.transpose(product.reshape(V, O, V), (1, 0, 2)).astype(jnp.bfloat16)

    cycle = lax.map(one_row, amplitudes)
    label_i = occupied_irreps[:IW]
    total = jnp.bitwise_xor(label_i[:, None, None, None], occupied_irreps[None, :, None, None])
    total = jnp.bitwise_xor(total, virtual_irreps[None, None, :, None])
    total = jnp.bitwise_xor(total, virtual_irreps[None, None, None, :])
    return jnp.where(total == 0, cycle, jnp.zeros_like(cycle))
```

```python
import functools

import jax
import jax.numpy as jnp
from jax import lax
from jax.experimental import pallas as pl
from jax.experimental.pallas import tpu as pltpu
from jax.sharding import PartitionSpec as P

BF = jnp.bfloat16
F32 = jnp.float32
CAP = 64
NX = NY = 4
NZ = 8


def shift(step):
    return [(z, (z + step) % NZ) for z in range(NZ)]


def hop(first, step):
    pairs = []
    for x in range(NX):
        for y in range(NY):
            for c in range(2):
                along_x = (c == 0) == first
                to_x = (x + step) % NX if along_x else x
                to_y = y if along_x else (y + step) % NY
                pairs.append(((x * NY + y) * 2 + c, (to_x * NY + to_y) * 2 + c))
    return pairs


SWAP = [(d, d ^ 1) for d in range(2 * NX * NY)]


def positions(labels):
    before = jnp.sum((labels[None, :] < labels[:, None]).astype(jnp.int32), axis=1)
    return jnp.arange(labels.shape[0], dtype=jnp.int32) - before


def pick_matrix(pos_ref, base_ref):
    v = pos_ref.shape[1]
    rows = lax.broadcasted_iota(jnp.int32, (CAP, v), 0) + base_ref[0]
    return (rows == pos_ref[...]).astype(F32).astype(BF)


def pack_w_kernel(base_ref, pos_ref, w_ref, out_ref):
    pick = pick_matrix(pos_ref, base_ref)
    for k in range(w_ref.shape[0]):
        out_ref[k] = jnp.dot(pick, w_ref[k], preferred_element_type=F32).astype(BF)


def pack_w(pos, base, w):
    nk, v, _ = w.shape
    return pl.pallas_call(
        pack_w_kernel,
        out_shape=jax.ShapeDtypeStruct((nk, CAP, v), BF),
        in_specs=[
            pl.BlockSpec(memory_space=pltpu.SMEM),
            pl.BlockSpec(memory_space=pltpu.VMEM),
            pl.BlockSpec(memory_space=pltpu.VMEM),
        ],
        out_specs=pl.BlockSpec(memory_space=pltpu.VMEM),
        compiler_params=pltpu.CompilerParams(vmem_limit_bytes=32 * 2**20),
        name="pack_w",
    )(base, pos, w)


def pack_t_kernel(base_ref, pos_ref, t_ref, out_ref):
    pick = pick_matrix(pos_ref, base_ref)
    none = jnp.zeros_like(pick)
    ni, na, v = t_ref.shape
    half = ni // 2
    low = t_ref[:half].reshape(half * na, v)
    high = t_ref[half:].reshape(half * na, v)
    dims = (((1,), (1,)), ((), ()))
    both = lax.dot_general(low, jnp.concatenate([pick, none], 0), dims, preferred_element_type=F32)
    both += lax.dot_general(high, jnp.concatenate([none, pick], 0), dims, preferred_element_type=F32)
    out_ref[...] = both.astype(BF).reshape(half, na, 2 * CAP)


def pack_t(pos, base, t):
    ni, na, v = t.shape
    return pl.pallas_call(
        pack_t_kernel,
        out_shape=jax.ShapeDtypeStruct((ni // 2, na, 2 * CAP), BF),
        in_specs=[
            pl.BlockSpec(memory_space=pltpu.SMEM),
            pl.BlockSpec(memory_space=pltpu.VMEM),
            pl.BlockSpec(memory_space=pltpu.VMEM),
        ],
        out_specs=pl.BlockSpec(memory_space=pltpu.VMEM),
        compiler_params=pltpu.CompilerParams(vmem_limit_bytes=32 * 2**20),
        name="pack_t",
    )(base, pos, t)


def gather_w(d):
    half = d.shape[0] // 2
    right = left = d
    pieces = [d]
    for _ in range(3):
        right = lax.ppermute(right, "su", shift(1))
        left = lax.ppermute(left, "su", shift(-1))
        pieces += [right, left]
    pieces.append(lax.ppermute(right[:half], "su", shift(1)))
    pieces.append(lax.ppermute(left[half:], "su", shift(-1)))
    return pieces


OFFSETS = (0, 1, -1, 2, -2, 3, -3, 4)


def line(own, first):
    ahead, back = hop(first, 1), hop(first, -1)
    half = own.shape[0] // 2
    r = lax.ppermute(own, "tr", ahead)
    l = lax.ppermute(own, "tr", back)
    ro = lax.ppermute(r[:half], "tr", ahead)
    lo = lax.ppermute(l[half:], "tr", back)
    return own, l, jnp.concatenate([ro, lo], 0), r


def gather_t(t):
    pieces = jnp.stack(line(t, True))
    plane = jnp.concatenate(line(pieces, False), 0)
    return plane, lax.ppermute(plane, "tr", SWAP)


def accumulate(own_ref, other_ref, d_refs, d_cat, t_cat):
    v = d_refs[0].shape[2]
    nk = d_refs[0].shape[0]
    half_i, na = own_ref.shape[1], own_ref.shape[2]
    rows = half_i * na
    tr = lax.axis_index("tr")
    z = lax.axis_index("su")
    x, y, core = tr // (2 * NY), (tr // 2) % NY, tr % 2
    depth = nk * CAP
    for n, off in enumerate(OFFSETS):
        if n < 7:
            d_cat[n * depth : (n + 1) * depth] = d_refs[n][...].reshape(depth, v)
        else:
            d_cat[n * depth : n * depth + depth // 2] = d_refs[7][...].reshape(depth // 2, v)
            d_cat[n * depth + depth // 2 :] = d_refs[8][...].reshape(depth // 2, v)
        block = (z - off + NZ) % NZ
        for e in range(nk // 2):
            chip = block * (nk // 2) + e
            dx = (chip // NY - x + NX) % NX
            dy = (chip % NY - y + NY) % NY
            x_first = dy * NX + dx
            y_first = dx * NY + dy
            own_at = jnp.where(core == 0, x_first, y_first)
            other_at = jnp.where(core == 0, y_first, x_first)
            mine = own_ref[own_at].reshape(rows, 2 * CAP)
            theirs = other_ref[other_at].reshape(rows, 2 * CAP)
            even = jnp.where(core == 0, mine, theirs)
            odd = jnp.where(core == 0, theirs, mine)
            at = n * depth + e * 2 * CAP
            t_cat[0, :, at : at + 2 * CAP] = jnp.concatenate([even[:, :CAP], odd[:, :CAP]], 1)
            t_cat[1, :, at : at + 2 * CAP] = jnp.concatenate([even[:, CAP:], odd[:, CAP:]], 1)


def final_kernel(occ_ref, plane_ref, own_ref, other_ref, *refs):
    d_refs, (out_ref, d_cat, t_cat) = refs[:9], refs[9:]
    accumulate(own_ref, other_ref, d_refs, d_cat, t_cat)
    half_i, na = own_ref.shape[1], own_ref.shape[2]
    label_j = occ_ref[lax.axis_index("tr")]
    step = 2
    for h in range(2):
        for i0 in range(0, half_i, step):
            rows = t_cat[h, i0 * na : (i0 + step) * na, :]
            sums = jnp.dot(rows, d_cat[...], preferred_element_type=F32)
            for u in range(step):
                i = h * half_i + i0 + u
                keep = plane_ref[...] == jnp.bitwise_xor(occ_ref[i], label_j)
                out_ref[i] = jnp.where(keep, sums[u * na : (u + 1) * na], 0.0).astype(BF)


def sum_kernel(own_ref, other_ref, *refs):
    d_refs, (acc_ref, out_ref, d_cat, t_cat) = refs[:9], refs[9:]
    accumulate(own_ref, other_ref, d_refs, d_cat, t_cat)
    half_i, na = own_ref.shape[1], own_ref.shape[2]
    for h in range(2):
        for i in range(half_i):
            rows = t_cat[h, i * na : (i + 1) * na, :]
            out_ref[h * half_i + i] = acc_ref[h * half_i + i] + jnp.dot(rows, d_cat[...], preferred_element_type=F32)


def scratch(t_own, d):
    half_i, na = t_own.shape[1], t_own.shape[2]
    depth = NZ * d.shape[0] * CAP
    return [pltpu.VMEM((depth, d.shape[2]), BF), pltpu.VMEM((2, half_i * na, depth), BF)]


def body(amplitudes, integrals, occupied_irreps, virtual_irreps):
    ni, _, na, v = amplitudes.shape
    t = amplitudes.reshape(ni, na, v)
    w = integrals.reshape(integrals.shape[0], v, v)
    pos = positions(virtual_irreps)
    pos_row = pos.reshape(1, v)

    def one_pass(base):
        base = jnp.full((1,), base, jnp.int32)
        d = pack_w(pos_row, base, w)
        p = pack_t(pos_row, base, t)
        pieces = gather_w(d)
        own, other = gather_t(p)
        return own, other, pieces

    start_a = lax.axis_index("su") * na
    labels_a = lax.dynamic_slice_in_dim(virtual_irreps, start_a, na, 0)
    plane = jnp.bitwise_xor(labels_a[:, None], virtual_irreps[None, :])
    own, other, pieces = one_pass(0)
    vmem = pl.BlockSpec(memory_space=pltpu.VMEM)
    flops = 2 * ni * na * v * NZ * w.shape[0] * CAP
    fast = pl.pallas_call(
        final_kernel,
        out_shape=jax.ShapeDtypeStruct((ni, na, v), BF),
        in_specs=[pl.BlockSpec(memory_space=pltpu.SMEM)] + [vmem] * 12,
        out_specs=vmem,
        scratch_shapes=scratch(own, pieces[0]),
        compiler_params=pltpu.CompilerParams(vmem_limit_bytes=40 * 2**20),
        cost_estimate=pl.CostEstimate(flops=flops, bytes_accessed=6 * 2**20, transcendentals=0),
        name="contract",
    )(occupied_irreps, plane, own, other, *pieces)

    def all_windows():
        def window(n, acc):
            own, other, pieces = one_pass(n * CAP)
            return pl.pallas_call(
                sum_kernel,
                out_shape=jax.ShapeDtypeStruct((ni, na, v), F32),
                in_specs=[vmem] * 12,
                out_specs=vmem,
                scratch_shapes=scratch(own, pieces[0]),
                compiler_params=pltpu.CompilerParams(vmem_limit_bytes=40 * 2**20),
                name="contract_window",
            )(own, other, *pieces, acc)

        windows = jnp.max(pos) // CAP + 1
        acc = lax.fori_loop(0, windows, window, jnp.zeros((ni, na, v), F32))
        label_j = occupied_irreps[lax.axis_index("tr")]
        parity = jnp.bitwise_xor(occupied_irreps[:ni, None, None], label_j)
        keep = jnp.bitwise_xor(parity, plane[None]) == 0
        return jnp.where(keep, acc.astype(BF), jnp.zeros((), BF))

    out = lax.cond(jnp.max(pos) < CAP, lambda: fast, all_windows)
    return out.reshape(ni, 1, na, v)


def solution(mesh):
    return jax.shard_map(
        body,
        mesh=mesh,
        in_specs=(P(None, "tr", "su", None), P("su", None, "tr", None), P(), P()),
        out_specs=P(None, "tr", "su", None),
        check_vma=False,
    )
```

```python
import math

import jax
import jax.numpy as jnp
from jax import lax
from jax.experimental import pallas as pl
from jax.experimental.pallas import tpu as pltpu
from jax.sharding import PartitionSpec as P

BF = jnp.bfloat16
F32 = jnp.float32
CAP = 64
NX = NY = 4
NZ = 8


ODD_LINKS = [(z, (z + 1) % NZ if z % 2 else (z - 1) % NZ) for z in range(NZ)]
EVEN_LINKS = [(z, (z - 1) % NZ if z % 2 else (z + 1) % NZ) for z in range(NZ)]


def line(first, flip):
    pairs = []
    for x in range(NX):
        for y in range(NY):
            for c in range(2):
                along_x = (c == 0) == first
                to_x = x ^ flip if along_x else x
                to_y = y if along_x else y ^ flip
                pairs.append(((x * NY + y) * 2 + c, (to_x * NY + to_y) * 2 + c))
    return pairs


SWAP = [(d, d ^ 1) for d in range(2 * NX * NY)]


def pick_matrix(pos, base_ref):
    rows = lax.broadcasted_iota(jnp.int32, (CAP, pos.shape[1]), 0) + base_ref[0]
    return (rows == pos).astype(F32).astype(BF)


def pack_t_kernel(base_ref, labels_ref, t_ref, out_ref, pos_ref, fits_ref):
    labels = labels_ref[...]
    pos = lax.broadcasted_iota(jnp.int32, labels.shape, 1)
    for g in range(1, 8):
        first = jnp.sum((labels < g).astype(F32), axis=1, keepdims=True).astype(jnp.int32)
        pos -= jnp.where(labels == g, first, 0)
    pos_ref[...] = pos
    fits_ref[0] = jnp.max(pos) + 1
    pick = pick_matrix(pos, base_ref)
    none = jnp.zeros_like(pick)
    ni, na, v = t_ref.shape
    half = ni // 2
    low = t_ref[:half].reshape(half * na, v)
    high = t_ref[half:].reshape(half * na, v)
    dims = (((1,), (1,)), ((), ()))
    both = lax.dot_general(low, jnp.concatenate([pick, none], 0), dims, preferred_element_type=F32)
    both += lax.dot_general(high, jnp.concatenate([none, pick], 0), dims, preferred_element_type=F32)
    out_ref[0] = both.astype(BF).reshape(half, na, 2 * CAP)


def pack_w_kernel(base_ref, pos_ref, w_ref, keep_ref, give_ref):
    pick = pick_matrix(pos_ref[...], base_ref)
    core = lax.axis_index("tr") % 2
    for e in range(keep_ref.shape[1]):
        keep_ref[0, e] = jnp.dot(pick, w_ref[2 * e + core], preferred_element_type=F32).astype(BF)
        give_ref[0, e] = jnp.dot(pick, w_ref[2 * e + 1 - core], preferred_element_type=F32).astype(BF)


SMEM = pl.BlockSpec(memory_space=pltpu.SMEM)
VMEM = pl.BlockSpec(memory_space=pltpu.VMEM)
ANY = pl.BlockSpec(memory_space=pl.ANY)


def pack_t(labels_row, base, t):
    ni, na, v = t.shape
    return pl.pallas_call(
        pack_t_kernel,
        out_shape=(
            jax.ShapeDtypeStruct((1, ni // 2, na, 2 * CAP), BF),
            jax.ShapeDtypeStruct(labels_row.shape, jnp.int32),
            jax.ShapeDtypeStruct((1,), jnp.int32),
        ),
        in_specs=[SMEM, VMEM, VMEM],
        out_specs=(VMEM, VMEM, SMEM),
        compiler_params=pltpu.CompilerParams(vmem_limit_bytes=8 * 2**20),
        cost_estimate=pl.CostEstimate(flops=0, bytes_accessed=2 * 2**20, transcendentals=0),
        name="pack_t",
    )(base, labels_row, t)


def pack_w(pos, base, w):
    nk, v, _ = w.shape
    part = jax.ShapeDtypeStruct((1, nk // 2, CAP, v), BF)
    return pl.pallas_call(
        pack_w_kernel,
        out_shape=(part, part),
        in_specs=[SMEM, VMEM, VMEM],
        out_specs=(VMEM, VMEM),
        compiler_params=pltpu.CompilerParams(vmem_limit_bytes=8 * 2**20),
        cost_estimate=pl.CostEstimate(flops=0, bytes_accessed=4 * 2**20, transcendentals=0),
        name="pack_w",
    )(base, pos, w)


OFFSETS = (0, 1, -1, 2, -2, 3, -3, 4)


def join_kernel(*refs):
    out_ref = refs[-1]
    at = 0
    for ref in refs[:-1]:
        out_ref[at : at + ref.shape[0]] = ref[...]
        at += ref.shape[0]


def join(name, *parts):
    shape = (sum(p.shape[0] for p in parts), *parts[0].shape[1:])
    size = 2 * 4 * math.prod(shape)
    return pl.pallas_call(
        join_kernel,
        out_shape=jax.ShapeDtypeStruct(shape, parts[0].dtype),
        in_specs=[VMEM] * len(parts),
        out_specs=VMEM,
        compiler_params=pltpu.CompilerParams(vmem_limit_bytes=8 * 2**20),
        cost_estimate=pl.CostEstimate(flops=0, bytes_accessed=size, transcendentals=0),
        name=name,
    )(*parts)


def lines(piece, first):
    return [lax.ppermute(piece, "tr", line(first, flip)) for flip in (1, 2, 3)]


def gather(keep, give, t):
    rows = lines(t, True)
    d = join("join_w", keep, lax.ppermute(give, "tr", SWAP))
    a1 = lax.ppermute(d, "su", ODD_LINKS)
    b1 = lax.ppermute(d, "su", EVEN_LINKS)
    row = join("join_row", t, *rows)
    planes = lines(row, False)
    a2 = lax.ppermute(b1, "su", ODD_LINKS)
    b2 = lax.ppermute(a1, "su", EVEN_LINKS)
    a3 = lax.ppermute(b2, "su", ODD_LINKS)
    b3 = lax.ppermute(a2, "su", EVEN_LINKS)
    a4 = lax.ppermute(b3[:1], "su", ODD_LINKS)
    b4 = lax.ppermute(a3[1:], "su", EVEN_LINKS)
    a4, b4 = lax.optimization_barrier((a4, b4))
    return [row, *planes], [d, a1, b1, a2, b2, a3, b3], a4, b4


def first_kernel(*refs):
    t_refs, d_refs, (own_ref, other_ref, rest_ref, t_all, t_cat, d_cat, sems) = refs[:4], refs[4:-7], refs[-7:]
    copies = [pltpu.make_async_copy(t_ref, t_all.at[NX * n : NX * n + NX], sems.at[n]) for n, t_ref in enumerate(t_refs)]
    for copy in copies:
        copy.start()
    _, ne, cap, v = d_refs[0].shape
    half_i, na = t_all.shape[1:3]
    rows = half_i * na
    wide = ne * cap
    for n, d_ref in enumerate(d_refs):
        for j in range(2):
            d_cat[j, n * wide : (n + 1) * wide] = d_ref[j].reshape(wide, v)
    tr = lax.axis_index("tr")
    z = lax.axis_index("su")
    x, y, core = tr // (2 * NY), (tr // 2) % NY, tr % 2
    way = 1 - 2 * (z % 2)
    for copy in copies:
        copy.wait()
    for n, off in enumerate(OFFSETS):
        block = (z - off * way + NZ) % NZ
        pair = []
        for e in range(ne):
            chip = block * ne + e
            dx = jnp.bitwise_xor(chip // NY, x)
            dy = jnp.bitwise_xor(chip % NY, y)
            at = jnp.where(core == 0, dy * NX + dx, dx * NY + dy)
            pair.append(t_all[at].reshape(rows, 2 * CAP))
        for h in range(2):
            lanes = slice(h * CAP, (h + 1) * CAP)
            both = jnp.concatenate([pair[0][:, lanes], pair[1][:, lanes]], 1)
            if n < len(d_refs):
                t_cat[h, :, n * wide : (n + 1) * wide] = both
            else:
                rest_ref[h] = both
    for h in range(2):
        other_ref[h] = jnp.dot(t_cat[h], d_cat[1], preferred_element_type=F32)
        own_ref[h] = jnp.dot(t_cat[h], d_cat[0], preferred_element_type=F32)


def first_part(t_parts, d_parts):
    chips, half_i, na, lanes = t_parts[0].shape
    _, ne, cap, v = d_parts[0].shape
    rows = half_i * na
    wide = ne * cap
    depth = len(d_parts) * wide
    sums = jax.ShapeDtypeStruct((2, rows, v), F32)
    return pl.pallas_call(
        first_kernel,
        out_shape=(sums, sums, jax.ShapeDtypeStruct((2, rows, wide), BF)),
        in_specs=[ANY] * len(t_parts) + [VMEM] * len(d_parts),
        out_specs=(VMEM, VMEM, VMEM),
        scratch_shapes=[
            pltpu.VMEM((len(t_parts) * chips, half_i, na, lanes), BF),
            pltpu.VMEM((2, rows, depth), BF),
            pltpu.VMEM((2, depth, v), BF),
            pltpu.SemaphoreType.DMA((len(t_parts),)),
        ],
        compiler_params=pltpu.CompilerParams(vmem_limit_bytes=20 * 2**20),
        cost_estimate=pl.CostEstimate(flops=8 * rows * v * depth, bytes_accessed=8 * 2**20, transcendentals=0),
        name="first_part",
    )(*t_parts, *d_parts)


def block_sum(sums_ref, rest_ref, d_ref, h):
    _, ne, cap, v = d_ref.shape
    return sums_ref[h] + jnp.dot(rest_ref[h], d_ref[0].reshape(ne * cap, v), preferred_element_type=F32)


def other_kernel(other_ref, rest_ref, d_ref, out_ref):
    for h in range(2):
        out_ref[h] = block_sum(other_ref, rest_ref, d_ref, h)


def other_part(other, rest, d):
    return pl.pallas_call(
        other_kernel,
        out_shape=jax.ShapeDtypeStruct(other.shape, F32),
        in_specs=[VMEM] * 3,
        out_specs=VMEM,
        compiler_params=pltpu.CompilerParams(vmem_limit_bytes=8 * 2**20),
        name="other_part",
    )(other, rest, d)


def last_kernel(occ_ref, labels_ref, fits_ref, own_ref, got_ref, rest_ref, d_ref, out_ref, flag_ref):
    flag_ref[0] = (fits_ref[0] <= CAP).astype(jnp.int32)
    label_j = occ_ref[lax.axis_index("tr")]
    half_i = out_ref.shape[0] // 2
    na, v = out_ref.shape[1:]
    labels = labels_ref[...]
    place = lax.broadcasted_iota(jnp.int32, (na, v), 0) + lax.axis_index("su") * na
    here = lax.broadcasted_iota(jnp.int32, (na, v), 1) == place
    labels_a = jnp.sum(jnp.where(here, labels, 0).astype(F32), axis=1, keepdims=True).astype(jnp.int32)
    plane = jnp.bitwise_xor(labels_a, labels)
    for h in range(2):
        sums = block_sum(own_ref, rest_ref, d_ref, h) + got_ref[h]
        for u in range(half_i):
            i = h * half_i + u
            keep = plane == jnp.bitwise_xor(occ_ref[i], label_j)
            out_ref[i] = jnp.where(keep, sums[u * na : (u + 1) * na], 0.0).astype(BF)


def window_kernel(total_ref, own_ref, got_ref, rest_ref, d_ref, out_ref):
    for h in range(2):
        out_ref[h] = total_ref[h] + block_sum(own_ref, rest_ref, d_ref, h) + got_ref[h]


def body(amplitudes, integrals, occupied_irreps, virtual_irreps):
    ni, _, na, v = amplitudes.shape
    t = amplitudes.reshape(ni, na, v)
    w = integrals.reshape(integrals.shape[0], v, v)
    labels_row = virtual_irreps.reshape(1, v)

    def one_pass(base):
        base = jnp.full((1,), base, jnp.int32)
        packed, pos, width = pack_t(labels_row, base, t)
        keep, give = pack_w(pos, base, w)
        t_parts, d_parts, a4, b4 = gather(keep, give, packed)
        own, other, rest = first_part(t_parts, d_parts)
        got = lax.ppermute(other_part(other, rest, b4), "tr", SWAP)
        return own, got, rest, a4, width

    own, got, rest, a4, width = one_pass(0)
    fast, fits = pl.pallas_call(
        last_kernel,
        out_shape=(jax.ShapeDtypeStruct((ni, na, v), BF), jax.ShapeDtypeStruct((1,), jnp.int32)),
        in_specs=[SMEM, VMEM, SMEM] + [VMEM] * 4,
        out_specs=(VMEM, SMEM),
        compiler_params=pltpu.CompilerParams(vmem_limit_bytes=8 * 2**20),
        name="last_part",
    )(occupied_irreps, labels_row, width, own, got, rest, a4)

    def all_windows():
        def window(n, total):
            own, got, rest, a4, _ = one_pass(n * CAP)
            return pl.pallas_call(
                window_kernel,
                out_shape=jax.ShapeDtypeStruct(total.shape, F32),
                in_specs=[VMEM] * 5,
                out_specs=VMEM,
                compiler_params=pltpu.CompilerParams(vmem_limit_bytes=16 * 2**20),
                name="window_part",
            )(total, own, got, rest, a4)

        windows = (width[0] + CAP - 1) // CAP
        total = lax.fori_loop(0, windows, window, jnp.zeros(own.shape, F32))
        label_j = occupied_irreps[lax.axis_index("tr")]
        labels_a = lax.dynamic_slice_in_dim(virtual_irreps, lax.axis_index("su") * na, na, 0)
        parity = jnp.bitwise_xor(occupied_irreps[:ni, None, None], label_j)
        parity = jnp.bitwise_xor(parity, labels_a[None, :, None])
        keep = jnp.bitwise_xor(parity, virtual_irreps[None, None, :]) == 0
        return jnp.where(keep, total.reshape(ni, na, v).astype(BF), jnp.zeros((), BF))

    out = lax.cond(fits[0] == 1, lambda: fast, all_windows)
    return out.reshape(ni, 1, na, v)


def solution(mesh):
    return jax.shard_map(
        body,
        mesh=mesh,
        in_specs=(P(None, "tr", "su", None), P("su", None, "tr", None), P(), P()),
        out_specs=P(None, "tr", "su", None),
        check_vma=False,
    )
```

```python
import functools
import math

import jax
import jax.numpy as jnp
from jax import lax
from jax.experimental import pallas as pl
from jax.experimental.pallas import tpu as pltpu
from jax.sharding import PartitionSpec as P

BF = jnp.bfloat16
F32 = jnp.float32
IW = 16
CAP = 64
NX = NY = 4
NZ = 8


ODD_LINKS = [(z, (z + 1) % NZ if z % 2 else (z - 1) % NZ) for z in range(NZ)]
EVEN_LINKS = [(z, (z - 1) % NZ if z % 2 else (z + 1) % NZ) for z in range(NZ)]


def line(first, flip):
    pairs = []
    for x in range(NX):
        for y in range(NY):
            for c in range(2):
                along_x = (c == 0) == first
                to_x = x ^ flip if along_x else x
                to_y = y if along_x else y ^ flip
                pairs.append(((x * NY + y) * 2 + c, (to_x * NY + to_y) * 2 + c))
    return pairs


EVEN_LINKS_CROSSED = [(d * NZ + z, (d ^ 1) * NZ + to) for d in range(2 * NX * NY) for z, to in EVEN_LINKS]
SWAP = [(d, d ^ 1) for d in range(2 * NX * NY)]


def pick_matrix(pos, base):
    rows = lax.broadcasted_iota(jnp.int32, (CAP, pos.shape[1]), 0) + base
    return (rows == pos).astype(F32).astype(BF)


def group_positions(labels):
    pos = lax.broadcasted_iota(jnp.int32, labels.shape, 1)
    for g in range(1, 8):
        first = jnp.sum((labels < g).astype(F32), axis=1, keepdims=True).astype(jnp.int32)
        pos -= jnp.where(labels == g, first, 0)
    return pos


def give_kernel(window, labels_ref, w_ref, give_ref, pos_ref, width_ref, l_all, w_all, sems):
    base = 0 if window is None else window[0] * CAP
    ne = give_ref.shape[1]
    other = 1 - lax.axis_index("tr") % 2
    fetch_l = pltpu.make_async_copy(labels_ref, l_all, sems.at[ne])
    fetch_w = [pltpu.make_async_copy(w_ref.at[2 * e + other], w_all.at[e], sems.at[e]) for e in range(ne)]
    fetch_l.start()
    for copy in fetch_w:
        copy.start()
    fetch_l.wait()
    pos = group_positions(l_all[...].reshape(1, l_all.shape[0]))
    pos_ref[...] = pos
    width_ref[...] = jnp.full(width_ref.shape, 1, jnp.int32) + jnp.max(pos, axis=1, keepdims=True)
    pick = pick_matrix(pos, base)
    for e in range(ne):
        fetch_w[e].wait()
        give_ref[0, e] = jnp.dot(pick, w_all[e], preferred_element_type=F32).astype(BF)


def keep_kernel(window, pos_ref, t_ref, w_ref, row_ref, keep_ref, t_all, w_all, sems):
    base = 0 if window is None else window[0] * CAP
    ne = keep_ref.shape[1]
    core = lax.axis_index("tr") % 2
    fetch_w = [pltpu.make_async_copy(w_ref.at[2 * e + core], w_all.at[e], sems.at[e]) for e in range(ne)]
    fetch_t = pltpu.make_async_copy(t_ref, t_all, sems.at[ne])
    for copy in fetch_w:
        copy.start()
    fetch_t.start()
    pick = pick_matrix(pos_ref[...], base)
    none = jnp.zeros_like(pick)
    for e in range(ne):
        fetch_w[e].wait()
        keep_ref[0, e] = jnp.dot(pick, w_all[e], preferred_element_type=F32).astype(BF)
    fetch_t.wait()
    ni, na, v = t_all.shape
    half = ni // 2
    low = t_all[:half].reshape(half * na, v)
    high = t_all[half:].reshape(half * na, v)
    dims = (((1,), (1,)), ((), ()))
    both = lax.dot_general(low, jnp.concatenate([pick, none], 0), dims, preferred_element_type=F32)
    both += lax.dot_general(high, jnp.concatenate([none, pick], 0), dims, preferred_element_type=F32)
    row_ref[0] = both.astype(BF).reshape(half, na, 2 * CAP)


def bits_kernel(occ_ref, labels_ref, bits_ref):
    na, v = bits_ref.shape
    labels = labels_ref[...].reshape(1, v)
    place = lax.broadcasted_iota(jnp.int32, (na, v), 0) + lax.axis_index("su") * na
    here = lax.broadcasted_iota(jnp.int32, (na, v), 1) == place
    labels_a = jnp.sum(jnp.where(here, labels, 0).astype(F32), axis=1, keepdims=True).astype(jnp.int32)
    plane = jnp.bitwise_xor(jnp.bitwise_xor(labels_a, labels), occ_ref[lax.axis_index("tr")])
    bits = jnp.zeros((na, v), jnp.int32)
    for i in range(IW):
        bits += jnp.where(plane == occ_ref[i], 1 << i, 0)
    bits_ref[...] = bits


SMEM = pl.BlockSpec(memory_space=pltpu.SMEM)
VMEM = pl.BlockSpec(memory_space=pltpu.VMEM)
ANY = pl.BlockSpec(memory_space=pl.ANY)


def windowed(kernel, window):
    if window is None:
        return functools.partial(kernel, None), [], []
    return kernel, [SMEM], [window]


def pack_give(window, labels, w):
    nk, v, _ = w.shape
    kernel, specs, args = windowed(give_kernel, window)
    return pl.pallas_call(
        kernel,
        out_shape=(
            jax.ShapeDtypeStruct((1, nk // 2, CAP, v), BF),
            jax.ShapeDtypeStruct((1, v), jnp.int32),
            jax.ShapeDtypeStruct((1, 128), jnp.int32),
        ),
        in_specs=specs + [ANY, ANY],
        out_specs=(VMEM, VMEM, VMEM),
        scratch_shapes=[
            pltpu.VMEM((v,), jnp.int32),
            pltpu.VMEM((nk // 2, v, v), BF),
            pltpu.SemaphoreType.DMA((nk // 2 + 1,)),
        ],
        compiler_params=pltpu.CompilerParams(vmem_limit_bytes=8 * 2**20),
        name="pack_give",
    )(*args, labels, w)


def pack_keep(window, pos, t, w):
    nk, v, _ = w.shape
    ni, na, _ = t.shape
    kernel, specs, args = windowed(keep_kernel, window)
    return pl.pallas_call(
        kernel,
        out_shape=(
            jax.ShapeDtypeStruct((1, ni // 2, na, 2 * CAP), BF),
            jax.ShapeDtypeStruct((1, nk // 2, CAP, v), BF),
        ),
        in_specs=specs + [VMEM, ANY, ANY],
        out_specs=(VMEM, VMEM),
        scratch_shapes=[
            pltpu.VMEM(t.shape, BF),
            pltpu.VMEM((nk // 2, v, v), BF),
            pltpu.SemaphoreType.DMA((nk // 2 + 1,)),
        ],
        compiler_params=pltpu.CompilerParams(vmem_limit_bytes=8 * 2**20),
        cost_estimate=pl.CostEstimate(flops=0, bytes_accessed=4 * 2**20, transcendentals=0),
        name="pack_keep",
    )(*args, pos, t, w)


def symmetric_bits(occupied, labels, na):
    return pl.pallas_call(
        bits_kernel,
        out_shape=jax.ShapeDtypeStruct((na, labels.shape[0]), jnp.int32),
        in_specs=[SMEM, VMEM],
        out_specs=VMEM,
        compiler_params=pltpu.CompilerParams(vmem_limit_bytes=4 * 2**20),
        name="bits",
    )(occupied, labels)


OFFSETS = (0, 1, -1, 2, -2, 3, -3, 4)


def join_kernel(*refs):
    out_ref = refs[-1]
    at = 0
    for ref in refs[:-1]:
        out_ref[at : at + ref.shape[0]] = ref[...]
        at += ref.shape[0]


def join(name, *parts):
    shape = (sum(p.shape[0] for p in parts), *parts[0].shape[1:])
    size = 2 * 4 * math.prod(shape)
    return pl.pallas_call(
        join_kernel,
        out_shape=jax.ShapeDtypeStruct(shape, parts[0].dtype),
        in_specs=[VMEM] * len(parts),
        out_specs=VMEM,
        compiler_params=pltpu.CompilerParams(vmem_limit_bytes=8 * 2**20),
        cost_estimate=pl.CostEstimate(flops=0, bytes_accessed=size, transcendentals=0),
        name=name,
    )(*parts)


def lines(piece, first):
    return [lax.ppermute(piece, "tr", line(first, flip)) for flip in (1, 2, 3)]


def gather(keep, got, t):
    rows = lines(t, True)
    d = join("join_w", keep, got)
    a1 = lax.ppermute(d, "su", ODD_LINKS)
    b1 = lax.ppermute(d, "su", EVEN_LINKS)
    row = join("join_row", t, *rows)
    planes = lines(row, False)
    a2 = lax.ppermute(b1, "su", ODD_LINKS)
    b2 = lax.ppermute(a1, "su", EVEN_LINKS)
    a3 = lax.ppermute(b2, "su", ODD_LINKS)
    b3 = lax.ppermute(a2, "su", EVEN_LINKS)
    a4 = lax.ppermute(b3[:1], "su", ODD_LINKS)
    b4 = lax.ppermute(a3[1:], ("tr", "su"), EVEN_LINKS_CROSSED)
    return [row, *planes], [d, a1, b1, a2, b2, a3, b3], a4, b4


def blocks(d_refs, j, d_cat):
    _, ne, cap, v = d_refs[0].shape
    wide = ne * cap
    for n, d_ref in enumerate(d_refs):
        d_cat[n * wide : (n + 1) * wide] = d_ref[j].reshape(wide, v)


def other_kernel(*refs):
    t_refs, d_refs, (other_ref, t_cat, rest_ref, t_all, d_cat, sems) = refs[:4], refs[4:-6], refs[-6:]
    copies = [pltpu.make_async_copy(t_ref, t_all.at[NX * n : NX * n + NX], sems.at[n]) for n, t_ref in enumerate(t_refs)]
    for copy in copies:
        copy.start()
    _, ne, cap, v = d_refs[0].shape
    half_i, na = t_all.shape[1:3]
    rows = half_i * na
    wide = ne * cap
    blocks(d_refs, 1, d_cat)
    tr = lax.axis_index("tr")
    z = lax.axis_index("su")
    x, y, core = tr // (2 * NY), (tr // 2) % NY, tr % 2
    way = 1 - 2 * (z % 2)
    for copy in copies:
        copy.wait()
    for n, off in enumerate(OFFSETS):
        block = (z - off * way + NZ) % NZ
        pair = []
        for e in range(ne):
            chip = block * ne + e
            dx = jnp.bitwise_xor(chip // NY, x)
            dy = jnp.bitwise_xor(chip % NY, y)
            at = jnp.where(core == 0, dy * NX + dx, dx * NY + dy)
            pair.append(t_all[at].reshape(rows, 2 * CAP))
        for h in range(2):
            lanes = slice(h * CAP, (h + 1) * CAP)
            both = jnp.concatenate([pair[0][:, lanes], pair[1][:, lanes]], 1)
            if n < len(d_refs):
                t_cat[h, :, n * wide : (n + 1) * wide] = both
            else:
                rest_ref[h] = both
    for h in range(2):
        other_ref[h] = jnp.dot(t_cat[h], d_cat[...], preferred_element_type=F32)


def other_part(t_parts, d_parts):
    chips, half_i, na, lanes = t_parts[0].shape
    _, ne, cap, v = d_parts[0].shape
    rows = half_i * na
    wide = ne * cap
    depth = len(d_parts) * wide
    return pl.pallas_call(
        other_kernel,
        out_shape=(
            jax.ShapeDtypeStruct((2, rows, v), F32),
            jax.ShapeDtypeStruct((2, rows, depth), BF),
            jax.ShapeDtypeStruct((2, rows, wide), BF),
        ),
        in_specs=[ANY] * len(t_parts) + [VMEM] * len(d_parts),
        out_specs=(VMEM, VMEM, VMEM),
        scratch_shapes=[
            pltpu.VMEM((len(t_parts) * chips, half_i, na, lanes), BF),
            pltpu.VMEM((depth, v), BF),
            pltpu.SemaphoreType.DMA((len(t_parts),)),
        ],
        compiler_params=pltpu.CompilerParams(vmem_limit_bytes=20 * 2**20),
        cost_estimate=pl.CostEstimate(flops=4 * rows * v * depth, bytes_accessed=6 * 2**20, transcendentals=0),
        name="other_part",
    )(*t_parts, *d_parts)


def own_kernel(t_cat, *refs):
    d_refs, (own_ref, d_cat) = refs[:-2], refs[-2:]
    blocks(d_refs, 0, d_cat)
    for h in range(2):
        own_ref[h] = jnp.dot(t_cat[h], d_cat[...], preferred_element_type=F32)


def own_part(t_cat, d_parts):
    _, rows, depth = t_cat.shape
    v = d_parts[0].shape[3]
    return pl.pallas_call(
        own_kernel,
        out_shape=jax.ShapeDtypeStruct((2, rows, v), F32),
        in_specs=[VMEM] * (1 + len(d_parts)),
        out_specs=VMEM,
        scratch_shapes=[pltpu.VMEM((depth, v), BF)],
        compiler_params=pltpu.CompilerParams(vmem_limit_bytes=12 * 2**20),
        cost_estimate=pl.CostEstimate(flops=4 * rows * v * depth, bytes_accessed=4 * 2**20, transcendentals=0),
        name="own_part",
    )(t_cat, *d_parts)


def total(h, own_ref, got_ref, rest_ref, rest_got_ref, a4_ref, b4_ref):
    _, ne, cap, v = a4_ref.shape
    left = jnp.concatenate([rest_ref[h], rest_got_ref[h]], 1)
    right = jnp.concatenate([a4_ref[0].reshape(ne * cap, v), b4_ref[0].reshape(ne * cap, v)], 0)
    return own_ref[h] + got_ref[h] + jnp.dot(left, right, preferred_element_type=F32)


def last_kernel(width_ref, bits_ref, *refs):
    parts, (out_ref, fits_ref) = refs[:-2], refs[-2:]
    fits_ref[0] = (width_ref[0, 0] <= CAP).astype(jnp.int32)
    half_i = out_ref.shape[0] // 2
    na = out_ref.shape[1]
    for h in range(2):
        sums = total(h, *parts)
        for u in range(half_i):
            i = h * half_i + u
            keep = jnp.bitwise_and(bits_ref[...], 1 << i) != 0
            out_ref[i] = jnp.where(keep, sums[u * na : (u + 1) * na], 0.0).astype(BF)


def window_kernel(before_ref, *refs):
    parts, out_ref = refs[:-1], refs[-1]
    for h in range(2):
        out_ref[h] = before_ref[h] + total(h, *parts)


def body(amplitudes, integrals, occupied_irreps, virtual_irreps):
    ni, _, na, v = amplitudes.shape
    t = amplitudes.reshape(ni, na, v)
    w = integrals.reshape(integrals.shape[0], v, v)

    def one_pass(window):
        give, pos, width = pack_give(window, virtual_irreps, w)
        got = lax.ppermute(give, "tr", SWAP)
        row, keep = pack_keep(window, pos, t, w)
        t_parts, d_parts, a4, b4 = gather(keep, got, row)
        other, t_cat, rest = other_part(t_parts, d_parts)
        other, a4, b4 = lax.optimization_barrier((other, a4, b4))
        got = lax.ppermute(other, "tr", SWAP)
        rest_got = lax.ppermute(rest, "tr", SWAP)
        own = own_part(t_cat, d_parts)
        return (own, got, rest, rest_got, a4, b4), width

    parts, width = one_pass(None)
    fast, fits = pl.pallas_call(
        last_kernel,
        out_shape=(jax.ShapeDtypeStruct((ni, na, v), BF), jax.ShapeDtypeStruct((1,), jnp.int32)),
        in_specs=[VMEM, VMEM] + [VMEM] * len(parts),
        out_specs=(VMEM, SMEM),
        compiler_params=pltpu.CompilerParams(vmem_limit_bytes=8 * 2**20),
        name="last_part",
    )(width, symmetric_bits(occupied_irreps, virtual_irreps, na), *parts)

    def all_windows():
        def window(n, before):
            parts, _ = one_pass(jnp.full((1,), n, jnp.int32))
            return pl.pallas_call(
                window_kernel,
                out_shape=jax.ShapeDtypeStruct(before.shape, F32),
                in_specs=[VMEM] * (1 + len(parts)),
                out_specs=VMEM,
                compiler_params=pltpu.CompilerParams(vmem_limit_bytes=16 * 2**20),
                name="window_part",
            )(before, *parts)

        windows = (width[0, 0] + CAP - 1) // CAP
        sums = lax.fori_loop(0, windows, window, jnp.zeros(parts[0].shape, F32))
        label_j = occupied_irreps[lax.axis_index("tr")]
        labels_a = lax.dynamic_slice_in_dim(virtual_irreps, lax.axis_index("su") * na, na, 0)
        parity = jnp.bitwise_xor(occupied_irreps[:ni, None, None], label_j)
        parity = jnp.bitwise_xor(parity, labels_a[None, :, None])
        keep = jnp.bitwise_xor(parity, virtual_irreps[None, None, :]) == 0
        return jnp.where(keep, sums.reshape(ni, na, v).astype(BF), jnp.zeros((), BF))

    out = lax.cond(fits[0] == 1, lambda: fast, all_windows)
    return out.reshape(ni, 1, na, v)


def solution(mesh):
    return jax.shard_map(
        body,
        mesh=mesh,
        in_specs=(P(None, "tr", "su", None), P("su", None, "tr", None), P(), P()),
        out_specs=P(None, "tr", "su", None),
        check_vma=False,
    )
```

```python
import functools
import math

import jax
import jax.numpy as jnp
from jax import lax
from jax.experimental import pallas as pl
from jax.experimental.pallas import tpu as pltpu
from jax.sharding import PartitionSpec as P

BF = jnp.bfloat16
F32 = jnp.float32
IW = 16
CAP = 64
NX = NY = 4
NZ = 8


ODD_LINKS = [(z, (z + 1) % NZ if z % 2 else (z - 1) % NZ) for z in range(NZ)]
EVEN_LINKS = [(z, (z - 1) % NZ if z % 2 else (z + 1) % NZ) for z in range(NZ)]


def line(first, flip):
    pairs = []
    for x in range(NX):
        for y in range(NY):
            for c in range(2):
                along_x = (c == 0) == first
                to_x = x ^ flip if along_x else x
                to_y = y if along_x else y ^ flip
                pairs.append(((x * NY + y) * 2 + c, (to_x * NY + to_y) * 2 + c))
    return pairs


EVEN_LINKS_CROSSED = [(d * NZ + z, (d ^ 1) * NZ + to) for d in range(2 * NX * NY) for z, to in EVEN_LINKS]
SWAP = [(d, d ^ 1) for d in range(2 * NX * NY)]


def pick_matrix(pos, base):
    rows = lax.broadcasted_iota(jnp.int32, (CAP, pos.shape[1]), 0) + base
    return (rows == pos).astype(F32).astype(BF)


def group_positions(labels):
    pos = lax.broadcasted_iota(jnp.int32, labels.shape, 1)
    for g in range(1, 8):
        first = jnp.sum((labels < g).astype(F32), axis=1, keepdims=True).astype(jnp.int32)
        pos -= jnp.where(labels == g, first, 0)
    return pos


def give_kernel(window, labels_ref, w_ref, give_ref, pos_ref, width_ref, l_all, w_all, sems):
    base = 0 if window is None else window[0] * CAP
    ne = give_ref.shape[1]
    other = 1 - lax.axis_index("tr") % 2
    fetch_l = pltpu.make_async_copy(labels_ref, l_all, sems.at[ne])
    fetch_w = [pltpu.make_async_copy(w_ref.at[2 * e + other], w_all.at[e], sems.at[e]) for e in range(ne)]
    fetch_l.start()
    for copy in fetch_w:
        copy.start()
    fetch_l.wait()
    pos = group_positions(l_all[...].reshape(1, l_all.shape[0]))
    pos_ref[...] = pos
    width_ref[...] = jnp.full(width_ref.shape, 1, jnp.int32) + jnp.max(pos, axis=1, keepdims=True)
    pick = pick_matrix(pos, base)
    for e in range(ne):
        fetch_w[e].wait()
        give_ref[0, e] = jnp.dot(pick, w_all[e], preferred_element_type=F32).astype(BF)


def keep_kernel(window, pos_ref, t_ref, w_ref, row_ref, keep_ref, t_all, w_all, sems):
    base = 0 if window is None else window[0] * CAP
    ne = keep_ref.shape[1]
    core = lax.axis_index("tr") % 2
    fetch_w = [pltpu.make_async_copy(w_ref.at[2 * e + core], w_all.at[e], sems.at[e]) for e in range(ne)]
    fetch_t = pltpu.make_async_copy(t_ref, t_all, sems.at[ne])
    for copy in fetch_w:
        copy.start()
    fetch_t.start()
    pick = pick_matrix(pos_ref[...], base)
    none = jnp.zeros_like(pick)
    for e in range(ne):
        fetch_w[e].wait()
        keep_ref[0, e] = jnp.dot(pick, w_all[e], preferred_element_type=F32).astype(BF)
    fetch_t.wait()
    ni, na, v = t_all.shape
    half = ni // 2
    low = t_all[:half].reshape(half * na, v)
    high = t_all[half:].reshape(half * na, v)
    dims = (((1,), (1,)), ((), ()))
    both = lax.dot_general(low, jnp.concatenate([pick, none], 0), dims, preferred_element_type=F32)
    both += lax.dot_general(high, jnp.concatenate([none, pick], 0), dims, preferred_element_type=F32)
    row_ref[0] = both.astype(BF).reshape(half, na, 2 * CAP)


def prepare_kernel(occ_ref, labels_ref, pos_ref, bits_ref, pick_own_ref, pick_other_ref, spread_ref, expand_ref):
    na, v = bits_ref.shape
    labels = labels_ref[...].reshape(1, v)
    pos = pos_ref[...]
    tr = lax.axis_index("tr")
    place = lax.broadcasted_iota(jnp.int32, (na, v), 0) + lax.axis_index("su") * na
    here = lax.broadcasted_iota(jnp.int32, (na, v), 1) == place
    labels_a = jnp.sum(jnp.where(here, labels, 0).astype(F32), axis=1, keepdims=True).astype(jnp.int32)
    plane = jnp.bitwise_xor(jnp.bitwise_xor(labels_a, labels), occ_ref[tr])
    bits = jnp.zeros((na, v), jnp.int32)
    for i in range(IW):
        bits += jnp.where(plane == occ_ref[i], 1 << i, 0)
    bits_ref[...] = bits
    rows_a = jnp.broadcast_to(labels_a, pick_own_ref.shape[1:])
    for i in range(IW):
        for ref, j in ((pick_own_ref, tr), (pick_other_ref, jnp.bitwise_xor(tr, 1))):
            ref[i] = jnp.right_shift(jnp.bitwise_xor(rows_a, jnp.bitwise_xor(occ_ref[i], occ_ref[j])), 1)
    wide = lax.broadcasted_iota(jnp.int32, spread_ref.shape, 0) == labels * CAP + pos
    spread_ref[...] = wide.astype(F32).astype(BF)
    pair = lax.broadcasted_iota(jnp.int32, expand_ref.shape, 0) == jnp.bitwise_and(labels, 1) * CAP + pos
    expand_ref[...] = pair.astype(F32).astype(BF)


SMEM = pl.BlockSpec(memory_space=pltpu.SMEM)
VMEM = pl.BlockSpec(memory_space=pltpu.VMEM)
ANY = pl.BlockSpec(memory_space=pl.ANY)


def windowed(kernel, window):
    if window is None:
        return functools.partial(kernel, None), [], []
    return kernel, [SMEM], [window]


def pack_give(window, labels, w):
    nk, v, _ = w.shape
    kernel, specs, args = windowed(give_kernel, window)
    return pl.pallas_call(
        kernel,
        out_shape=(
            jax.ShapeDtypeStruct((1, nk // 2, CAP, v), BF),
            jax.ShapeDtypeStruct((1, v), jnp.int32),
            jax.ShapeDtypeStruct((1, 128), jnp.int32),
        ),
        in_specs=specs + [ANY, ANY],
        out_specs=(VMEM, VMEM, VMEM),
        scratch_shapes=[
            pltpu.VMEM((v,), jnp.int32),
            pltpu.VMEM((nk // 2, v, v), BF),
            pltpu.SemaphoreType.DMA((nk // 2 + 1,)),
        ],
        compiler_params=pltpu.CompilerParams(vmem_limit_bytes=8 * 2**20),
        name="pack_give",
    )(*args, labels, w)


def pack_keep(window, pos, t, w):
    nk, v, _ = w.shape
    ni, na, _ = t.shape
    kernel, specs, args = windowed(keep_kernel, window)
    return pl.pallas_call(
        kernel,
        out_shape=(
            jax.ShapeDtypeStruct((1, ni // 2, na, 2 * CAP), BF),
            jax.ShapeDtypeStruct((1, nk // 2, CAP, v), BF),
        ),
        in_specs=specs + [VMEM, ANY, ANY],
        out_specs=(VMEM, VMEM),
        scratch_shapes=[
            pltpu.VMEM(t.shape, BF),
            pltpu.VMEM((nk // 2, v, v), BF),
            pltpu.SemaphoreType.DMA((nk // 2 + 1,)),
        ],
        compiler_params=pltpu.CompilerParams(vmem_limit_bytes=8 * 2**20),
        cost_estimate=pl.CostEstimate(flops=0, bytes_accessed=4 * 2**20, transcendentals=0),
        name="pack_keep",
    )(*args, pos, t, w)


def prepare(occupied, labels, pos, na):
    v = labels.shape[0]
    pick = jax.ShapeDtypeStruct((IW, na, 2 * CAP), jnp.int32)
    return pl.pallas_call(
        prepare_kernel,
        out_shape=(
            jax.ShapeDtypeStruct((na, v), jnp.int32),
            pick,
            pick,
            jax.ShapeDtypeStruct((8 * CAP, v), BF),
            jax.ShapeDtypeStruct((2 * CAP, v), BF),
        ),
        in_specs=[SMEM, VMEM, VMEM],
        out_specs=(VMEM,) * 5,
        compiler_params=pltpu.CompilerParams(vmem_limit_bytes=8 * 2**20),
        name="prepare",
    )(occupied, labels, pos)


OFFSETS = (0, 1, -1, 2, -2, 3, -3, 4)


def join_kernel(*refs):
    out_ref = refs[-1]
    at = 0
    for ref in refs[:-1]:
        out_ref[at : at + ref.shape[0]] = ref[...]
        at += ref.shape[0]


def join(name, *parts):
    shape = (sum(p.shape[0] for p in parts), *parts[0].shape[1:])
    size = 2 * 4 * math.prod(shape)
    return pl.pallas_call(
        join_kernel,
        out_shape=jax.ShapeDtypeStruct(shape, parts[0].dtype),
        in_specs=[VMEM] * len(parts),
        out_specs=VMEM,
        compiler_params=pltpu.CompilerParams(vmem_limit_bytes=8 * 2**20),
        cost_estimate=pl.CostEstimate(flops=0, bytes_accessed=size, transcendentals=0),
        name=name,
    )(*parts)


def lines(piece, first):
    return [lax.ppermute(piece, "tr", line(first, flip)) for flip in (1, 2, 3)]


def gather(keep, got, t):
    rows = lines(t, True)
    d = join("join_w", keep, got)
    a1 = lax.ppermute(d, "su", ODD_LINKS)
    b1 = lax.ppermute(d, "su", EVEN_LINKS)
    row = join("join_row", t, *rows)
    planes = lines(row, False)
    a2 = lax.ppermute(b1, "su", ODD_LINKS)
    b2 = lax.ppermute(a1, "su", EVEN_LINKS)
    a3 = lax.ppermute(b2, "su", ODD_LINKS)
    b3 = lax.ppermute(a2, "su", EVEN_LINKS)
    a4 = lax.ppermute(b3[:1], "su", ODD_LINKS)
    b4 = lax.ppermute(a3[1:], ("tr", "su"), EVEN_LINKS_CROSSED)
    return [row, *planes], [d, a1, b1, a2, b2, a3, b3], a4, b4


def blocks(d_refs, j, d_cat):
    _, ne, cap, v = d_refs[0].shape
    wide = ne * cap
    for n, d_ref in enumerate(d_refs):
        d_cat[n * wide : (n + 1) * wide] = d_ref[j].reshape(wide, v)


def other_kernel(*refs):
    t_refs, d_refs, (other_ref, t_cat, rest_ref, t_all, d_cat, sems) = refs[:4], refs[4:-6], refs[-6:]
    copies = [pltpu.make_async_copy(t_ref, t_all.at[NX * n : NX * n + NX], sems.at[n]) for n, t_ref in enumerate(t_refs)]
    for copy in copies:
        copy.start()
    _, ne, cap, v = d_refs[0].shape
    half_i, na = t_all.shape[1:3]
    rows = half_i * na
    wide = ne * cap
    blocks(d_refs, 1, d_cat)
    tr = lax.axis_index("tr")
    z = lax.axis_index("su")
    x, y, core = tr // (2 * NY), (tr // 2) % NY, tr % 2
    way = 1 - 2 * (z % 2)
    for copy in copies:
        copy.wait()
    for n, off in enumerate(OFFSETS):
        block = (z - off * way + NZ) % NZ
        pair = []
        for e in range(ne):
            chip = block * ne + e
            dx = jnp.bitwise_xor(chip // NY, x)
            dy = jnp.bitwise_xor(chip % NY, y)
            at = jnp.where(core == 0, dy * NX + dx, dx * NY + dy)
            pair.append(t_all[at].reshape(rows, 2 * CAP))
        for h in range(2):
            lanes = slice(h * CAP, (h + 1) * CAP)
            both = jnp.concatenate([pair[0][:, lanes], pair[1][:, lanes]], 1)
            if n < len(d_refs):
                t_cat[h, :, n * wide : (n + 1) * wide] = both
            else:
                rest_ref[h] = both
    for h in range(2):
        other_ref[h] = jnp.dot(t_cat[h], d_cat[...], preferred_element_type=F32)


def other_part(t_parts, d_parts):
    chips, half_i, na, lanes = t_parts[0].shape
    _, ne, cap, v = d_parts[0].shape
    rows = half_i * na
    wide = ne * cap
    depth = len(d_parts) * wide
    return pl.pallas_call(
        other_kernel,
        out_shape=(
            jax.ShapeDtypeStruct((2, rows, v), F32),
            jax.ShapeDtypeStruct((2, rows, depth), BF),
            jax.ShapeDtypeStruct((2, rows, wide), BF),
        ),
        in_specs=[ANY] * len(t_parts) + [VMEM] * len(d_parts),
        out_specs=(VMEM, VMEM, VMEM),
        scratch_shapes=[
            pltpu.VMEM((len(t_parts) * chips, half_i, na, lanes), BF),
            pltpu.VMEM((depth, v), BF),
            pltpu.SemaphoreType.DMA((len(t_parts),)),
        ],
        compiler_params=pltpu.CompilerParams(vmem_limit_bytes=20 * 2**20),
        cost_estimate=pl.CostEstimate(flops=4 * rows * v * depth, bytes_accessed=6 * 2**20, transcendentals=0),
        name="other_part",
    )(*t_parts, *d_parts)


def own_kernel(t_cat, *refs):
    d_refs, (own_ref, d_cat) = refs[:-2], refs[-2:]
    blocks(d_refs, 0, d_cat)
    for h in range(2):
        own_ref[h] = jnp.dot(t_cat[h], d_cat[...], preferred_element_type=F32)


def own_part(t_cat, d_parts):
    _, rows, depth = t_cat.shape
    v = d_parts[0].shape[3]
    return pl.pallas_call(
        own_kernel,
        out_shape=jax.ShapeDtypeStruct((2, rows, v), F32),
        in_specs=[VMEM] * (1 + len(d_parts)),
        out_specs=VMEM,
        scratch_shapes=[pltpu.VMEM((depth, v), BF)],
        compiler_params=pltpu.CompilerParams(vmem_limit_bytes=12 * 2**20),
        cost_estimate=pl.CostEstimate(flops=4 * rows * v * depth, bytes_accessed=4 * 2**20, transcendentals=0),
        name="own_part",
    )(t_cat, *d_parts)


def total(h, own_ref, got_ref, rest_ref, rest_got_ref, a4_ref, b4_ref):
    _, ne, cap, v = a4_ref.shape
    left = jnp.concatenate([rest_ref[h], rest_got_ref[h]], 1)
    right = jnp.concatenate([a4_ref[0].reshape(ne * cap, v), b4_ref[0].reshape(ne * cap, v)], 0)
    return own_ref[h] + got_ref[h] + jnp.dot(left, right, preferred_element_type=F32)


def spread_kernel(spread_ref, *refs):
    d_refs, outs = refs[:-2], refs[-2:]
    _, ne, cap, v = d_refs[0].shape
    dims = (((1,), (1,)), ((), ()))
    for j in range(2):
        for n, d_ref in enumerate(d_refs):
            block = d_ref[j].reshape(ne * cap, v)
            wide = lax.dot_general(block, spread_ref[...], dims, preferred_element_type=F32)
            outs[j][n * ne : (n + 1) * ne] = wide.astype(BF).reshape(ne, cap, -1)
        outs[j][len(d_refs) * ne :] = jnp.zeros((ne, cap, spread_ref.shape[0]), BF)


def spread_blocks(spread, d_parts):
    _, ne, cap, v = d_parts[0].shape
    out = jax.ShapeDtypeStruct((NZ * ne, cap, spread.shape[0]), BF)
    return pl.pallas_call(
        spread_kernel,
        out_shape=(out, out),
        in_specs=[VMEM] * (1 + len(d_parts)),
        out_specs=(VMEM, VMEM),
        compiler_params=pltpu.CompilerParams(vmem_limit_bytes=8 * 2**20),
        cost_estimate=pl.CostEstimate(
            flops=4 * NZ * ne * cap * v * spread.shape[0], bytes_accessed=4 * 2**20, transcendentals=0
        ),
        name="spread",
    )(spread, *d_parts)


def block_at(first, second):
    tr = lax.axis_index("tr")
    z = lax.axis_index("su")
    x, y, core = tr // (2 * NY), (tr // 2) % NY, tr % 2
    to_x = jnp.bitwise_xor(x, jnp.where(core == 0, first, second))
    to_y = jnp.bitwise_xor(y, jnp.where(core == 0, second, first))
    ahead = (z - (2 * to_x + to_y // 2)) * (1 - 2 * (z % 2))
    hops = (ahead + 2 * NZ) % NZ
    arrival = jnp.where(hops == 0, 0, jnp.where(hops <= NZ // 2, 2 * hops - 1, 2 * (NZ - hops)))
    return 2 * arrival + to_y % 2


def pair_lanes(one, two, h):
    lanes = slice(h * CAP, (h + 1) * CAP)
    return jnp.concatenate([one[:, lanes], two[:, lanes]], 1)


def flat(piece):
    return piece.reshape(piece.shape[0] * piece.shape[1], piece.shape[2])


def early_kernel(*refs):
    t_refs, (d_own, d_other, own_ref, other_ref, t_cat, d_cat) = refs[:-6], refs[-6:]
    lanes = 2 * CAP
    for second, t_ref in enumerate(t_refs):
        for p in range(NX // 2):
            one, two = flat(t_ref[2 * p]), flat(t_ref[2 * p + 1])
            at = (second * (NX // 2) + p) * lanes
            for h in range(2):
                t_cat[h, :, at : at + lanes] = pair_lanes(one, two, h)
            for u in range(2):
                src = block_at(2 * p + u, second)
                d_cat[0, at + u * CAP : at + (u + 1) * CAP] = d_own[src]
                d_cat[1, at + u * CAP : at + (u + 1) * CAP] = d_other[src]
    for j, ref in enumerate((own_ref, other_ref)):
        for h in range(2):
            ref[h] = jnp.dot(t_cat[h], d_cat[j], preferred_element_type=F32)


def early_sums(t_parts, d_own, d_other):
    chips, half_i, na, lanes = t_parts[0].shape
    rows = half_i * na
    depth = len(t_parts) * chips * CAP
    wide = d_own.shape[2]
    out = jax.ShapeDtypeStruct((2, rows, wide), F32)
    return pl.pallas_call(
        early_kernel,
        out_shape=(out, out),
        in_specs=[VMEM] * (len(t_parts) + 2),
        out_specs=(VMEM, VMEM),
        scratch_shapes=[pltpu.VMEM((2, rows, depth), BF), pltpu.VMEM((2, depth, wide), BF)],
        compiler_params=pltpu.CompilerParams(vmem_limit_bytes=16 * 2**20),
        cost_estimate=pl.CostEstimate(flops=8 * rows * wide * depth, bytes_accessed=6 * 2**20, transcendentals=0),
        name="early_sums",
    )(*t_parts, d_own, d_other)


def keep_pair(sums, pick):
    lanes = 2 * CAP
    out = sums[:, :lanes]
    for g in range(1, 4):
        out = jnp.where(pick == g, sums[:, g * lanes : (g + 1) * lanes], out)
    return out


def late_blocks(d_ref, d_cat):
    for first in range(NX):
        d_cat[first * CAP : (first + 1) * CAP] = d_ref[block_at(first, NX - 1)]


def other_pair_kernel(pick_ref, *refs):
    t_refs, (sums_ref, d_ref, other_ref, late_ref, rest_ref, d_cat) = refs[:NX], refs[NX:]
    last = t_refs[-1]
    lanes = 2 * CAP
    for p in range(NX // 2):
        one, two = flat(last[2 * p]), flat(last[2 * p + 1])
        for h in range(2):
            late_ref[h, :, p * lanes : (p + 1) * lanes] = pair_lanes(one, two, h)
    late_blocks(d_ref, d_cat)
    ni, na = other_ref.shape[:2]
    half_i = ni // 2
    for h in range(2):
        sums = sums_ref[h] + jnp.dot(late_ref[h], d_cat[...], preferred_element_type=F32)
        for u in range(half_i):
            i = h * half_i + u
            other_ref[i] = keep_pair(sums[u * na : (u + 1) * na], pick_ref[i])
    tr = lax.axis_index("tr")
    far = (lax.axis_index("su") + NZ // 2) % NZ
    x, y, core = tr // (2 * NY), (tr // 2) % NY, tr % 2
    pair = []
    for e in range(2):
        dx = jnp.bitwise_xor(far // 2, x)
        dy = jnp.bitwise_xor(2 * (far % 2) + e, y)
        first = jnp.where(core == 0, dx, dy)
        second = jnp.where(core == 0, dy, dx)
        piece = t_refs[0][first]
        for n in range(1, NX):
            piece = jnp.where(second == n, t_refs[n][first], piece)
        pair.append(flat(piece))
    for h in range(2):
        rest_ref[h] = pair_lanes(*pair, h)


def other_pair(pick, t_parts, sums, d):
    chips, half_i, na, lanes = t_parts[0].shape
    rows = half_i * na
    return pl.pallas_call(
        other_pair_kernel,
        out_shape=(
            jax.ShapeDtypeStruct(pick.shape, F32),
            jax.ShapeDtypeStruct((2, rows, chips * CAP), BF),
            jax.ShapeDtypeStruct((2, rows, lanes), BF),
        ),
        in_specs=[VMEM] * (3 + len(t_parts)),
        out_specs=(VMEM, VMEM, VMEM),
        scratch_shapes=[pltpu.VMEM((chips * CAP, d.shape[2]), BF)],
        compiler_params=pltpu.CompilerParams(vmem_limit_bytes=12 * 2**20),
        cost_estimate=pl.CostEstimate(
            flops=4 * rows * d.shape[2] * chips * CAP, bytes_accessed=6 * 2**20, transcendentals=0
        ),
        name="other_pair",
    )(pick, *t_parts, sums, d)


def own_pair_kernel(pick_ref, spread_ref, sums_ref, late_ref, d_ref, rest_ref, rest_got_ref, a4_ref, b4_ref, own_ref, d_cat):
    _, ne, cap, v = a4_ref.shape
    depth = late_ref.shape[2]
    late_blocks(d_ref, d_cat)
    dims = (((1,), (1,)), ((), ()))
    for n, ref in enumerate((a4_ref, b4_ref)):
        wide = lax.dot_general(ref[0].reshape(ne * cap, v), spread_ref[...], dims, preferred_element_type=F32)
        d_cat[depth + n * ne * cap : depth + (n + 1) * ne * cap] = wide.astype(BF)
    ni, na = own_ref.shape[:2]
    half_i = ni // 2
    for h in range(2):
        left = jnp.concatenate([late_ref[h], rest_ref[h], rest_got_ref[h]], 1)
        sums = sums_ref[h] + jnp.dot(left, d_cat[...], preferred_element_type=F32)
        for u in range(half_i):
            i = h * half_i + u
            own_ref[i] = keep_pair(sums[u * na : (u + 1) * na], pick_ref[i])


def own_pair(pick, spread, sums, late, d, rest, rest_got, a4, b4):
    depth = late.shape[2] + 2 * rest.shape[2]
    return pl.pallas_call(
        own_pair_kernel,
        out_shape=jax.ShapeDtypeStruct(pick.shape, F32),
        in_specs=[VMEM] * 9,
        out_specs=VMEM,
        scratch_shapes=[pltpu.VMEM((depth, d.shape[2]), BF)],
        compiler_params=pltpu.CompilerParams(vmem_limit_bytes=12 * 2**20),
        cost_estimate=pl.CostEstimate(
            flops=4 * late.shape[1] * d.shape[2] * depth, bytes_accessed=4 * 2**20, transcendentals=0
        ),
        name="own_pair",
    )(pick, spread, sums, late, d, rest, rest_got, a4, b4)


def last_kernel(width_ref, bits_ref, expand_ref, own_ref, got_ref, out_ref, fits_ref):
    fits_ref[0] = (width_ref[0, 0] <= CAP).astype(jnp.int32)
    ni, na, lanes = own_ref.shape
    sums = (own_ref[...] + got_ref[...]).astype(BF).reshape(ni * na, lanes)
    wide = jnp.dot(sums, expand_ref[...], preferred_element_type=F32)
    for i in range(ni):
        keep = jnp.bitwise_and(bits_ref[...], 1 << i) != 0
        out_ref[i] = jnp.where(keep, wide[i * na : (i + 1) * na], 0.0).astype(BF)


def window_kernel(before_ref, *refs):
    parts, out_ref = refs[:-1], refs[-1]
    for h in range(2):
        out_ref[h] = before_ref[h] + total(h, *parts)


def body(amplitudes, integrals, occupied_irreps, virtual_irreps):
    ni, _, na, v = amplitudes.shape
    t = amplitudes.reshape(ni, na, v)
    w = integrals.reshape(integrals.shape[0], v, v)

    def one_pass(window):
        give, pos, width = pack_give(window, virtual_irreps, w)
        got = lax.ppermute(give, "tr", SWAP)
        row, keep = pack_keep(window, pos, t, w)
        return *gather(keep, got, row), pos, width

    t_parts, d_parts, a4, b4, pos, width = one_pass(None)
    bits, pick_own, pick_other, spread, expand = prepare(occupied_irreps, virtual_irreps, pos, na)
    d_own, d_other = spread_blocks(spread, d_parts)
    sums_own, sums_other = early_sums(t_parts[:-1], d_own, d_other)
    other, t_late, rest = other_pair(pick_other, t_parts, sums_other, d_other)
    other, a4, b4 = lax.optimization_barrier((other, a4, b4))
    got = lax.ppermute(other, "tr", SWAP)
    rest_got = lax.ppermute(rest, "tr", SWAP)
    own = own_pair(pick_own, spread, sums_own, t_late, d_own, rest, rest_got, a4, b4)
    fast, fits = pl.pallas_call(
        last_kernel,
        out_shape=(jax.ShapeDtypeStruct((ni, na, v), BF), jax.ShapeDtypeStruct((1,), jnp.int32)),
        in_specs=[VMEM] * 5,
        out_specs=(VMEM, SMEM),
        compiler_params=pltpu.CompilerParams(vmem_limit_bytes=8 * 2**20),
        name="last_part",
    )(width, bits, expand, own, got)

    def all_windows():
        def window(n, before):
            t_parts, d_parts, a4, b4, _, _ = one_pass(jnp.full((1,), n, jnp.int32))
            other, t_cat, rest = other_part(t_parts, d_parts)
            got = lax.ppermute(other, "tr", SWAP)
            rest_got = lax.ppermute(rest, "tr", SWAP)
            parts = (own_part(t_cat, d_parts), got, rest, rest_got, a4, b4)
            return pl.pallas_call(
                window_kernel,
                out_shape=jax.ShapeDtypeStruct(before.shape, F32),
                in_specs=[VMEM] * (1 + len(parts)),
                out_specs=VMEM,
                compiler_params=pltpu.CompilerParams(vmem_limit_bytes=16 * 2**20),
                name="window_part",
            )(before, *parts)

        windows = (width[0, 0] + CAP - 1) // CAP
        sums = lax.fori_loop(0, windows, window, jnp.zeros((2, ni // 2 * na, v), F32))
        label_j = occupied_irreps[lax.axis_index("tr")]
        labels_a = lax.dynamic_slice_in_dim(virtual_irreps, lax.axis_index("su") * na, na, 0)
        parity = jnp.bitwise_xor(occupied_irreps[:ni, None, None], label_j)
        parity = jnp.bitwise_xor(parity, labels_a[None, :, None])
        keep = jnp.bitwise_xor(parity, virtual_irreps[None, None, :]) == 0
        return jnp.where(keep, sums.reshape(ni, na, v).astype(BF), jnp.zeros((), BF))

    out = lax.cond(fits[0] == 1, lambda: fast, all_windows)
    return out.reshape(ni, 1, na, v)


def solution(mesh):
    return jax.shard_map(
        body,
        mesh=mesh,
        in_specs=(P(None, "tr", "su", None), P("su", None, "tr", None), P(), P()),
        out_specs=P(None, "tr", "su", None),
        check_vma=False,
    )
```

```python
import functools
import math

import jax
import jax.numpy as jnp
from jax import lax
from jax.experimental import pallas as pl
from jax.experimental.pallas import tpu as pltpu
from jax.sharding import PartitionSpec as P

BF = jnp.bfloat16
F32 = jnp.float32
IW = 16
CAP = 64
NX = NY = 4
NZ = 8


ODD_LINKS = [(z, (z + 1) % NZ if z % 2 else (z - 1) % NZ) for z in range(NZ)]
EVEN_LINKS = [(z, (z - 1) % NZ if z % 2 else (z + 1) % NZ) for z in range(NZ)]


def line(first, flip):
    pairs = []
    for x in range(NX):
        for y in range(NY):
            for c in range(2):
                along_x = (c == 0) == first
                to_x = x ^ flip if along_x else x
                to_y = y if along_x else y ^ flip
                pairs.append(((x * NY + y) * 2 + c, (to_x * NY + to_y) * 2 + c))
    return pairs


SWAP = [(d, d ^ 1) for d in range(2 * NX * NY)]


def pick_matrix(pos, base):
    rows = lax.broadcasted_iota(jnp.int32, (CAP, pos.shape[1]), 0) + base
    return (rows == pos).astype(F32).astype(BF)


def group_positions(labels):
    pos = lax.broadcasted_iota(jnp.int32, labels.shape, 1)
    for g in range(1, 8):
        first = jnp.sum((labels < g).astype(F32), axis=1, keepdims=True).astype(jnp.int32)
        pos -= jnp.where(labels == g, first, 0)
    return pos


def give_kernel(window, labels_ref, w_ref, give_ref, pos_ref, width_ref, l_all, w_all, sems):
    base = 0 if window is None else window[0] * CAP
    ne = give_ref.shape[1]
    other = 1 - lax.axis_index("tr") % 2
    fetch_l = pltpu.make_async_copy(labels_ref, l_all, sems.at[ne])
    fetch_w = [pltpu.make_async_copy(w_ref.at[2 * e + other], w_all.at[e], sems.at[e]) for e in range(ne)]
    fetch_l.start()
    for copy in fetch_w:
        copy.start()
    fetch_l.wait()
    pos = group_positions(l_all[...].reshape(1, l_all.shape[0]))
    pos_ref[...] = pos
    width_ref[...] = jnp.full(width_ref.shape, 1, jnp.int32) + jnp.max(pos, axis=1, keepdims=True)
    pick = pick_matrix(pos, base)
    for e in range(ne):
        fetch_w[e].wait()
        give_ref[0, e] = jnp.dot(pick, w_all[e], preferred_element_type=F32).astype(BF)


def keep_kernel(window, pos_ref, t_ref, w_ref, row_ref, keep_ref, t_all, w_all, sems):
    base = 0 if window is None else window[0] * CAP
    ne = keep_ref.shape[1]
    core = lax.axis_index("tr") % 2
    fetch_w = [pltpu.make_async_copy(w_ref.at[2 * e + core], w_all.at[e], sems.at[e]) for e in range(ne)]
    fetch_t = pltpu.make_async_copy(t_ref, t_all, sems.at[ne])
    for copy in fetch_w:
        copy.start()
    fetch_t.start()
    pick = pick_matrix(pos_ref[...], base)
    none = jnp.zeros_like(pick)
    for e in range(ne):
        fetch_w[e].wait()
        keep_ref[0, e] = jnp.dot(pick, w_all[e], preferred_element_type=F32).astype(BF)
    fetch_t.wait()
    ni, na, v = t_all.shape
    half = ni // 2
    low = t_all[:half].reshape(half * na, v)
    high = t_all[half:].reshape(half * na, v)
    dims = (((1,), (1,)), ((), ()))
    both = lax.dot_general(low, jnp.concatenate([pick, none], 0), dims, preferred_element_type=F32)
    both += lax.dot_general(high, jnp.concatenate([none, pick], 0), dims, preferred_element_type=F32)
    row_ref[0] = both.astype(BF).reshape(half, na, 2 * CAP)


def prepare_kernel(occ_ref, labels_ref, pos_ref, bits_ref, pick_own_ref, pick_other_ref, spread_ref, expand_ref):
    na, v = bits_ref.shape
    labels = labels_ref[...].reshape(1, v)
    pos = pos_ref[...]
    tr = lax.axis_index("tr")
    place = lax.broadcasted_iota(jnp.int32, (na, v), 0) + lax.axis_index("su") * na
    here = lax.broadcasted_iota(jnp.int32, (na, v), 1) == place
    labels_a = jnp.sum(jnp.where(here, labels, 0).astype(F32), axis=1, keepdims=True).astype(jnp.int32)
    plane = jnp.bitwise_xor(jnp.bitwise_xor(labels_a, labels), occ_ref[tr])
    bits = jnp.zeros((na, v), jnp.int32)
    for i in range(IW):
        bits += jnp.where(plane == occ_ref[i], 1 << i, 0)
    bits_ref[...] = bits
    rows_a = jnp.broadcast_to(labels_a, pick_own_ref.shape[1:])
    for i in range(IW):
        for ref, j in ((pick_own_ref, tr), (pick_other_ref, jnp.bitwise_xor(tr, 1))):
            ref[i] = jnp.right_shift(jnp.bitwise_xor(rows_a, jnp.bitwise_xor(occ_ref[i], occ_ref[j])), 1)
    wide = lax.broadcasted_iota(jnp.int32, spread_ref.shape, 0) == labels * CAP + pos
    spread_ref[...] = wide.astype(F32).astype(BF)
    pair = lax.broadcasted_iota(jnp.int32, expand_ref.shape, 0) == jnp.bitwise_and(labels, 1) * CAP + pos
    expand_ref[...] = pair.astype(F32).astype(BF)


SMEM = pl.BlockSpec(memory_space=pltpu.SMEM)
VMEM = pl.BlockSpec(memory_space=pltpu.VMEM)
ANY = pl.BlockSpec(memory_space=pl.ANY)


def windowed(kernel, window):
    if window is None:
        return functools.partial(kernel, None), [], []
    return kernel, [SMEM], [window]


def pack_give(window, labels, w):
    nk, v, _ = w.shape
    kernel, specs, args = windowed(give_kernel, window)
    return pl.pallas_call(
        kernel,
        out_shape=(
            jax.ShapeDtypeStruct((1, nk // 2, CAP, v), BF),
            jax.ShapeDtypeStruct((1, v), jnp.int32),
            jax.ShapeDtypeStruct((1, 128), jnp.int32),
        ),
        in_specs=specs + [ANY, ANY],
        out_specs=(VMEM, VMEM, VMEM),
        scratch_shapes=[
            pltpu.VMEM((v,), jnp.int32),
            pltpu.VMEM((nk // 2, v, v), BF),
            pltpu.SemaphoreType.DMA((nk // 2 + 1,)),
        ],
        compiler_params=pltpu.CompilerParams(vmem_limit_bytes=8 * 2**20),
        name="pack_give",
    )(*args, labels, w)


def pack_keep(window, pos, t, w):
    nk, v, _ = w.shape
    ni, na, _ = t.shape
    kernel, specs, args = windowed(keep_kernel, window)
    return pl.pallas_call(
        kernel,
        out_shape=(
            jax.ShapeDtypeStruct((1, ni // 2, na, 2 * CAP), BF),
            jax.ShapeDtypeStruct((1, nk // 2, CAP, v), BF),
        ),
        in_specs=specs + [VMEM, ANY, ANY],
        out_specs=(VMEM, VMEM),
        scratch_shapes=[
            pltpu.VMEM(t.shape, BF),
            pltpu.VMEM((nk // 2, v, v), BF),
            pltpu.SemaphoreType.DMA((nk // 2 + 1,)),
        ],
        compiler_params=pltpu.CompilerParams(vmem_limit_bytes=8 * 2**20),
        cost_estimate=pl.CostEstimate(flops=0, bytes_accessed=4 * 2**20, transcendentals=0),
        name="pack_keep",
    )(*args, pos, t, w)


def prepare(occupied, labels, pos, na):
    v = labels.shape[0]
    pick = jax.ShapeDtypeStruct((IW, na, 2 * CAP), jnp.int32)
    return pl.pallas_call(
        prepare_kernel,
        out_shape=(
            jax.ShapeDtypeStruct((na, v), jnp.int32),
            pick,
            pick,
            jax.ShapeDtypeStruct((8 * CAP, v), BF),
            jax.ShapeDtypeStruct((2 * CAP, v), BF),
        ),
        in_specs=[SMEM, VMEM, VMEM],
        out_specs=(VMEM,) * 5,
        compiler_params=pltpu.CompilerParams(vmem_limit_bytes=8 * 2**20),
        name="prepare",
    )(occupied, labels, pos)


OFFSETS = (0, 1, -1, 2, -2, 3, -3, 4)


def join_kernel(*refs):
    out_ref = refs[-1]
    at = 0
    for ref in refs[:-1]:
        out_ref[at : at + ref.shape[0]] = ref[...]
        at += ref.shape[0]


def join(name, *parts):
    shape = (sum(p.shape[0] for p in parts), *parts[0].shape[1:])
    size = 2 * 4 * math.prod(shape)
    return pl.pallas_call(
        join_kernel,
        out_shape=jax.ShapeDtypeStruct(shape, parts[0].dtype),
        in_specs=[VMEM] * len(parts),
        out_specs=VMEM,
        compiler_params=pltpu.CompilerParams(vmem_limit_bytes=8 * 2**20),
        cost_estimate=pl.CostEstimate(flops=0, bytes_accessed=size, transcendentals=0),
        name=name,
    )(*parts)


def lines(piece, first):
    return [lax.ppermute(piece, "tr", line(first, flip)) for flip in (1, 2, 3)]


def gather(keep, got, t, beside=lambda parts: ()):
    rows = lines(t, True)
    d = join("join_w", keep, got)
    a1 = lax.ppermute(d, "su", ODD_LINKS)
    b1 = lax.ppermute(d, "su", EVEN_LINKS)
    row = join("join_row", t, *rows)
    planes = lines(row, False)
    a2 = lax.ppermute(b1, "su", ODD_LINKS)
    b2 = lax.ppermute(a1, "su", EVEN_LINKS)
    a3 = lax.ppermute(b2, "su", ODD_LINKS)
    b3 = lax.ppermute(a2, "su", EVEN_LINKS)
    extra, a3 = lax.optimization_barrier((beside([d, a1, b1, a2, b2]), a3))
    a4 = lax.ppermute(b3[:1], "su", ODD_LINKS)
    b4 = lax.ppermute(a3[1:], "su", EVEN_LINKS)
    return [row, *planes], [d, a1, b1, a2, b2, a3, b3], a4, b4, extra


def blocks(d_refs, j, d_cat):
    _, ne, cap, v = d_refs[0].shape
    wide = ne * cap
    for n, d_ref in enumerate(d_refs):
        d_cat[n * wide : (n + 1) * wide] = d_ref[j].reshape(wide, v)


def other_kernel(*refs):
    t_refs, d_refs, (other_ref, t_cat, rest_ref, t_all, d_cat, sems) = refs[:4], refs[4:-6], refs[-6:]
    copies = [pltpu.make_async_copy(t_ref, t_all.at[NX * n : NX * n + NX], sems.at[n]) for n, t_ref in enumerate(t_refs)]
    for copy in copies:
        copy.start()
    _, ne, cap, v = d_refs[0].shape
    half_i, na = t_all.shape[1:3]
    rows = half_i * na
    wide = ne * cap
    blocks(d_refs, 1, d_cat)
    tr = lax.axis_index("tr")
    z = lax.axis_index("su")
    x, y, core = tr // (2 * NY), (tr // 2) % NY, tr % 2
    way = 1 - 2 * (z % 2)
    for copy in copies:
        copy.wait()
    for n, off in enumerate(OFFSETS):
        block = (z - off * way + NZ) % NZ
        pair = []
        for e in range(ne):
            chip = block * ne + e
            dx = jnp.bitwise_xor(chip // NY, x)
            dy = jnp.bitwise_xor(chip % NY, y)
            at = jnp.where(core == 0, dy * NX + dx, dx * NY + dy)
            pair.append(t_all[at].reshape(rows, 2 * CAP))
        for h in range(2):
            lanes = slice(h * CAP, (h + 1) * CAP)
            both = jnp.concatenate([pair[0][:, lanes], pair[1][:, lanes]], 1)
            if n < len(d_refs):
                t_cat[h, :, n * wide : (n + 1) * wide] = both
            else:
                rest_ref[h] = both
    for h in range(2):
        other_ref[h] = jnp.dot(t_cat[h], d_cat[...], preferred_element_type=F32)


def other_part(t_parts, d_parts):
    chips, half_i, na, lanes = t_parts[0].shape
    _, ne, cap, v = d_parts[0].shape
    rows = half_i * na
    wide = ne * cap
    depth = len(d_parts) * wide
    return pl.pallas_call(
        other_kernel,
        out_shape=(
            jax.ShapeDtypeStruct((2, rows, v), F32),
            jax.ShapeDtypeStruct((2, rows, depth), BF),
            jax.ShapeDtypeStruct((2, rows, wide), BF),
        ),
        in_specs=[ANY] * len(t_parts) + [VMEM] * len(d_parts),
        out_specs=(VMEM, VMEM, VMEM),
        scratch_shapes=[
            pltpu.VMEM((len(t_parts) * chips, half_i, na, lanes), BF),
            pltpu.VMEM((depth, v), BF),
            pltpu.SemaphoreType.DMA((len(t_parts),)),
        ],
        compiler_params=pltpu.CompilerParams(vmem_limit_bytes=20 * 2**20),
        cost_estimate=pl.CostEstimate(flops=4 * rows * v * depth, bytes_accessed=6 * 2**20, transcendentals=0),
        name="other_part",
    )(*t_parts, *d_parts)


def own_kernel(t_cat, *refs):
    d_refs, (own_ref, d_cat) = refs[:-2], refs[-2:]
    blocks(d_refs, 0, d_cat)
    for h in range(2):
        own_ref[h] = jnp.dot(t_cat[h], d_cat[...], preferred_element_type=F32)


def own_part(t_cat, d_parts):
    _, rows, depth = t_cat.shape
    v = d_parts[0].shape[3]
    return pl.pallas_call(
        own_kernel,
        out_shape=jax.ShapeDtypeStruct((2, rows, v), F32),
        in_specs=[VMEM] * (1 + len(d_parts)),
        out_specs=VMEM,
        scratch_shapes=[pltpu.VMEM((depth, v), BF)],
        compiler_params=pltpu.CompilerParams(vmem_limit_bytes=12 * 2**20),
        cost_estimate=pl.CostEstimate(flops=4 * rows * v * depth, bytes_accessed=4 * 2**20, transcendentals=0),
        name="own_part",
    )(t_cat, *d_parts)


def far_sum(h, sums_ref, rest_ref, d_ref):
    _, ne, cap, v = d_ref.shape
    return sums_ref[h] + jnp.dot(rest_ref[h], d_ref[0].reshape(ne * cap, v), preferred_element_type=F32)


def far_kernel(sums_ref, rest_ref, d_ref, out_ref):
    for h in range(2):
        out_ref[h] = far_sum(h, sums_ref, rest_ref, d_ref)


def far_part(sums, rest, d):
    return pl.pallas_call(
        far_kernel,
        out_shape=jax.ShapeDtypeStruct(sums.shape, F32),
        in_specs=[VMEM] * 3,
        out_specs=VMEM,
        compiler_params=pltpu.CompilerParams(vmem_limit_bytes=8 * 2**20),
        name="far_part",
    )(sums, rest, d)


def spread_kernel(spread_ref, *refs):
    d_refs, (own_ref, other_ref, d_cat) = refs[:-3], refs[-3:]
    dims = (((1,), (1,)), ((), ()))
    for j, ref in enumerate((own_ref, other_ref)):
        blocks(d_refs, j, d_cat)
        wide = lax.dot_general(d_cat[...], spread_ref[...], dims, preferred_element_type=F32)
        ref[...] = wide.astype(BF).reshape(ref.shape)


def spread_blocks(spread, d_parts):
    _, ne, cap, v = d_parts[0].shape
    count = len(d_parts) * ne
    out = jax.ShapeDtypeStruct((count, cap, spread.shape[0]), BF)
    return pl.pallas_call(
        spread_kernel,
        out_shape=(out, out),
        in_specs=[VMEM] * (1 + len(d_parts)),
        out_specs=(VMEM, VMEM),
        scratch_shapes=[pltpu.VMEM((count * cap, v), BF)],
        compiler_params=pltpu.CompilerParams(vmem_limit_bytes=8 * 2**20),
        cost_estimate=pl.CostEstimate(
            flops=4 * count * cap * v * spread.shape[0], bytes_accessed=4 * 2**20, transcendentals=0
        ),
        name="spread",
    )(spread, *d_parts)


def put_block(d_early, d_late, first, second, d_cat, at):
    src = block_at(first, second)
    early, late = d_early.shape[0], d_late.shape[0]
    near = d_early[jnp.minimum(src, early - 1)]
    far = d_late[jnp.clip(src - early, 0, late - 1)]
    far = jnp.where(src < early + late, far, jnp.zeros_like(far))
    d_cat[at : at + CAP] = jnp.where(src < early, near, far)


def block_at(first, second):
    tr = lax.axis_index("tr")
    z = lax.axis_index("su")
    x, y, core = tr // (2 * NY), (tr // 2) % NY, tr % 2
    to_x = jnp.bitwise_xor(x, jnp.where(core == 0, first, second))
    to_y = jnp.bitwise_xor(y, jnp.where(core == 0, second, first))
    ahead = (z - (2 * to_x + to_y // 2)) * (1 - 2 * (z % 2))
    hops = (ahead + 2 * NZ) % NZ
    arrival = jnp.where(hops == 0, 0, jnp.where(hops <= NZ // 2, 2 * hops - 1, 2 * (NZ - hops)))
    return 2 * arrival + to_y % 2


def pair_lanes(one, two, h):
    lanes = slice(h * CAP, (h + 1) * CAP)
    return jnp.concatenate([one[:, lanes], two[:, lanes]], 1)


def flat(piece):
    return piece.reshape(piece.shape[0] * piece.shape[1], piece.shape[2])


def early_kernel(*refs):
    t_refs, (d_early, d_late, other_ref, t_cat, d_cat) = refs[:-5], refs[-5:]
    lanes = 2 * CAP
    for second, t_ref in enumerate(t_refs):
        for p in range(NX // 2):
            one, two = flat(t_ref[2 * p]), flat(t_ref[2 * p + 1])
            at = (second * (NX // 2) + p) * lanes
            for h in range(2):
                t_cat[h, :, at : at + lanes] = pair_lanes(one, two, h)
            for u in range(2):
                put_block(d_early, d_late, 2 * p + u, second, d_cat, at + u * CAP)
    for h in range(2):
        other_ref[h] = jnp.dot(t_cat[h], d_cat[...], preferred_element_type=F32)


def early_sums(t_parts, d_other):
    chips, half_i, na, lanes = t_parts[0].shape
    rows = half_i * na
    depth = len(t_parts) * chips * CAP
    wide = d_other[0].shape[2]
    return pl.pallas_call(
        early_kernel,
        out_shape=(jax.ShapeDtypeStruct((2, rows, wide), F32), jax.ShapeDtypeStruct((2, rows, depth), BF)),
        in_specs=[VMEM] * (len(t_parts) + 2),
        out_specs=(VMEM, VMEM),
        scratch_shapes=[pltpu.VMEM((depth, wide), BF)],
        compiler_params=pltpu.CompilerParams(vmem_limit_bytes=16 * 2**20),
        cost_estimate=pl.CostEstimate(flops=4 * rows * wide * depth, bytes_accessed=6 * 2**20, transcendentals=0),
        name="early_sums",
    )(*t_parts, *d_other)


def keep_pair(sums, pick):
    lanes = 2 * CAP
    out = sums[:, :lanes]
    for g in range(1, 4):
        out = jnp.where(pick == g, sums[:, g * lanes : (g + 1) * lanes], out)
    return out


def other_pair_kernel(pick_ref, *refs):
    t_refs, (sums_ref, d_early, d_late, other_ref, late_ref, rest_ref, d_cat) = refs[:NX], refs[NX:]
    last = t_refs[-1]
    lanes = 2 * CAP
    for p in range(NX // 2):
        one, two = flat(last[2 * p]), flat(last[2 * p + 1])
        for h in range(2):
            late_ref[h, :, p * lanes : (p + 1) * lanes] = pair_lanes(one, two, h)
    for first in range(NX):
        put_block(d_early, d_late, first, NX - 1, d_cat, first * CAP)
    ni, na = other_ref.shape[:2]
    half_i = ni // 2
    for h in range(2):
        sums = sums_ref[h] + jnp.dot(late_ref[h], d_cat[...], preferred_element_type=F32)
        for u in range(half_i):
            i = h * half_i + u
            other_ref[i] = keep_pair(sums[u * na : (u + 1) * na], pick_ref[i])
    tr = lax.axis_index("tr")
    far = (lax.axis_index("su") + NZ // 2) % NZ
    x, y, core = tr // (2 * NY), (tr // 2) % NY, tr % 2
    pair = []
    for e in range(2):
        dx = jnp.bitwise_xor(far // 2, x)
        dy = jnp.bitwise_xor(2 * (far % 2) + e, y)
        first = jnp.where(core == 0, dx, dy)
        second = jnp.where(core == 0, dy, dx)
        piece = t_refs[0][first]
        for n in range(1, NX):
            piece = jnp.where(second == n, t_refs[n][first], piece)
        pair.append(flat(piece))
    for h in range(2):
        rest_ref[h] = pair_lanes(*pair, h)


def other_pair(pick, t_parts, sums, d):
    chips, half_i, na, lanes = t_parts[0].shape
    rows = half_i * na
    return pl.pallas_call(
        other_pair_kernel,
        out_shape=(
            jax.ShapeDtypeStruct(pick.shape, F32),
            jax.ShapeDtypeStruct((2, rows, chips * CAP), BF),
            jax.ShapeDtypeStruct((2, rows, lanes), BF),
        ),
        in_specs=[VMEM] * (4 + len(t_parts)),
        out_specs=(VMEM, VMEM, VMEM),
        scratch_shapes=[pltpu.VMEM((chips * CAP, sums.shape[2]), BF)],
        compiler_params=pltpu.CompilerParams(vmem_limit_bytes=12 * 2**20),
        cost_estimate=pl.CostEstimate(
            flops=4 * rows * sums.shape[2] * chips * CAP, bytes_accessed=6 * 2**20, transcendentals=0
        ),
        name="other_pair",
    )(pick, *t_parts, sums, *d)


def spread_far(d_ref, spread_ref):
    _, ne, cap, v = d_ref.shape
    dims = (((1,), (1,)), ((), ()))
    wide = lax.dot_general(d_ref[0].reshape(ne * cap, v), spread_ref[...], dims, preferred_element_type=F32)
    return wide.astype(BF)


def far_pair_kernel(pick_ref, spread_ref, sums_ref, rest_ref, d_ref, out_ref):
    right = spread_far(d_ref, spread_ref)
    ni, na = out_ref.shape[:2]
    half_i = ni // 2
    for h in range(2):
        sums = jnp.dot(rest_ref[h], right, preferred_element_type=F32)
        for u in range(half_i):
            i = h * half_i + u
            out_ref[i] = sums_ref[i] + keep_pair(sums[u * na : (u + 1) * na], pick_ref[i])


def far_pair(pick, spread, sums, rest, d):
    return pl.pallas_call(
        far_pair_kernel,
        out_shape=jax.ShapeDtypeStruct(pick.shape, F32),
        in_specs=[VMEM] * 5,
        out_specs=VMEM,
        compiler_params=pltpu.CompilerParams(vmem_limit_bytes=8 * 2**20),
        name="far_pair",
    )(pick, spread, sums, rest, d)


def own_pair_kernel(
    pick_ref, spread_ref, t_cat, late_ref, d_early, d_late, rest_ref, far_ref, own_ref, left_cat, d_cat
):
    at = 0
    for ref in (t_cat, late_ref, rest_ref):
        left_cat[:, :, at : at + ref.shape[2]] = ref[...]
        at += ref.shape[2]
    for second in range(NX):
        for first in range(NX):
            put_block(d_early, d_late, first, second, d_cat, (second * NX + first) * CAP)
    d_cat[NX * NX * CAP :] = spread_far(far_ref, spread_ref)
    ni, na = own_ref.shape[:2]
    half_i = ni // 2
    for h in range(2):
        sums = jnp.dot(left_cat[h], d_cat[...], preferred_element_type=F32)
        for u in range(half_i):
            i = h * half_i + u
            own_ref[i] = keep_pair(sums[u * na : (u + 1) * na], pick_ref[i])


def own_pair(pick, spread, t_cat, late, d, rest, far):
    rows = late.shape[1]
    depth = t_cat.shape[2] + late.shape[2] + rest.shape[2]
    wide = d[0].shape[2]
    return pl.pallas_call(
        own_pair_kernel,
        out_shape=jax.ShapeDtypeStruct(pick.shape, F32),
        in_specs=[VMEM] * 8,
        out_specs=VMEM,
        scratch_shapes=[pltpu.VMEM((2, rows, depth), BF), pltpu.VMEM((depth, wide), BF)],
        compiler_params=pltpu.CompilerParams(vmem_limit_bytes=12 * 2**20),
        cost_estimate=pl.CostEstimate(flops=4 * rows * wide * depth, bytes_accessed=4 * 2**20, transcendentals=0),
        name="own_pair",
    )(pick, spread, t_cat, late, *d, rest, far)


def last_kernel(width_ref, bits_ref, expand_ref, own_ref, got_ref, out_ref, fits_ref):
    fits_ref[0] = (width_ref[0, 0] <= CAP).astype(jnp.int32)
    ni, na, lanes = own_ref.shape
    sums = (own_ref[...] + got_ref[...]).astype(BF).reshape(ni * na, lanes)
    wide = jnp.dot(sums, expand_ref[...], preferred_element_type=F32)
    for i in range(ni):
        keep = jnp.bitwise_and(bits_ref[...], 1 << i) != 0
        out_ref[i] = jnp.where(keep, wide[i * na : (i + 1) * na], 0.0).astype(BF)


def window_kernel(before_ref, own_ref, got_ref, rest_ref, d_ref, out_ref):
    for h in range(2):
        out_ref[h] = before_ref[h] + far_sum(h, own_ref, rest_ref, d_ref) + got_ref[h]


def body(amplitudes, integrals, occupied_irreps, virtual_irreps):
    ni, _, na, v = amplitudes.shape
    t = amplitudes.reshape(ni, na, v)
    w = integrals.reshape(integrals.shape[0], v, v)

    def pack(window):
        give, pos, width = pack_give(window, virtual_irreps, w)
        got = lax.ppermute(give, "tr", SWAP)
        row, keep = pack_keep(window, pos, t, w)
        return keep, got, row, pos, width

    keep, got, row, pos, width = pack(None)
    bits, pick_own, pick_other, spread, expand = prepare(occupied_irreps, virtual_irreps, pos, na)
    t_parts, d_parts, a4, b4, d_two = gather(keep, got, row, functools.partial(spread_blocks, spread))
    d_three = spread_blocks(spread, d_parts[5:])
    d_own, d_other = zip(d_two, d_three)
    sums_other, t_cat = early_sums(t_parts[:-1], d_other)
    other, t_late, rest = other_pair(pick_other, t_parts, sums_other, d_other)
    other, a4, b4 = lax.optimization_barrier((other, a4, b4))
    got = lax.ppermute(far_pair(pick_other, spread, other, rest, b4), "tr", SWAP)
    own = own_pair(pick_own, spread, t_cat, t_late, d_own, rest, a4)
    fast, fits = pl.pallas_call(
        last_kernel,
        out_shape=(jax.ShapeDtypeStruct((ni, na, v), BF), jax.ShapeDtypeStruct((1,), jnp.int32)),
        in_specs=[VMEM] * 5,
        out_specs=(VMEM, SMEM),
        compiler_params=pltpu.CompilerParams(vmem_limit_bytes=8 * 2**20),
        name="last_part",
    )(width, bits, expand, own, got)

    def all_windows():
        def window(n, before):
            keep, got, row, _, _ = pack(jnp.full((1,), n, jnp.int32))
            t_parts, d_parts, a4, b4, _ = gather(keep, got, row)
            other, t_cat, rest = other_part(t_parts, d_parts)
            got = lax.ppermute(far_part(other, rest, b4), "tr", SWAP)
            parts = (own_part(t_cat, d_parts), got, rest, a4)
            return pl.pallas_call(
                window_kernel,
                out_shape=jax.ShapeDtypeStruct(before.shape, F32),
                in_specs=[VMEM] * (1 + len(parts)),
                out_specs=VMEM,
                compiler_params=pltpu.CompilerParams(vmem_limit_bytes=16 * 2**20),
                name="window_part",
            )(before, *parts)

        windows = (width[0, 0] + CAP - 1) // CAP
        sums = lax.fori_loop(0, windows, window, jnp.zeros((2, ni // 2 * na, v), F32))
        label_j = occupied_irreps[lax.axis_index("tr")]
        labels_a = lax.dynamic_slice_in_dim(virtual_irreps, lax.axis_index("su") * na, na, 0)
        parity = jnp.bitwise_xor(occupied_irreps[:ni, None, None], label_j)
        parity = jnp.bitwise_xor(parity, labels_a[None, :, None])
        keep = jnp.bitwise_xor(parity, virtual_irreps[None, None, :]) == 0
        return jnp.where(keep, sums.reshape(ni, na, v).astype(BF), jnp.zeros((), BF))

    out = lax.cond(fits[0] == 1, lambda: fast, all_windows)
    return out.reshape(ni, 1, na, v)


def solution(mesh):
    return jax.shard_map(
        body,
        mesh=mesh,
        in_specs=(P(None, "tr", "su", None), P("su", None, "tr", None), P(), P()),
        out_specs=P(None, "tr", "su", None),
        check_vma=False,
    )
```

```python
import functools
import math

import jax
import jax.numpy as jnp
from jax import lax
from jax.experimental import pallas as pl
from jax.experimental.pallas import tpu as pltpu
from jax.sharding import PartitionSpec as P

BF = jnp.bfloat16
F32 = jnp.float32
IW = 16
CAP = 64
NX = NY = 4
NZ = 8


ODD_LINKS = [(z, (z + 1) % NZ if z % 2 else (z - 1) % NZ) for z in range(NZ)]
EVEN_LINKS = [(z, (z - 1) % NZ if z % 2 else (z + 1) % NZ) for z in range(NZ)]


def line(first, flip):
    pairs = []
    for x in range(NX):
        for y in range(NY):
            for c in range(2):
                along_x = (c == 0) == first
                to_x = x ^ flip if along_x else x
                to_y = y if along_x else y ^ flip
                pairs.append(((x * NY + y) * 2 + c, (to_x * NY + to_y) * 2 + c))
    return pairs


SWAP = [(d, d ^ 1) for d in range(2 * NX * NY)]


def pick_matrix(pos, base):
    rows = lax.broadcasted_iota(jnp.int32, (CAP, pos.shape[1]), 0) + base
    return (rows == pos).astype(F32).astype(BF)


def group_positions(labels):
    pos = lax.broadcasted_iota(jnp.int32, labels.shape, 1)
    for g in range(1, 8):
        first = jnp.sum((labels < g).astype(F32), axis=1, keepdims=True).astype(jnp.int32)
        pos -= jnp.where(labels == g, first, 0)
    return pos


def give_kernel(window, labels_ref, w_ref, give_ref, pos_ref, width_ref, l_all, w_all, sems):
    base = 0 if window is None else window[0] * CAP
    ne = give_ref.shape[1]
    other = 1 - lax.axis_index("tr") % 2
    fetch_l = pltpu.make_async_copy(labels_ref, l_all, sems.at[ne])
    fetch_w = [pltpu.make_async_copy(w_ref.at[2 * e + other], w_all.at[e], sems.at[e]) for e in range(ne)]
    fetch_l.start()
    for copy in fetch_w:
        copy.start()
    fetch_l.wait()
    pos = group_positions(l_all[...].reshape(1, l_all.shape[0]))
    pos_ref[...] = pos
    width_ref[...] = jnp.full(width_ref.shape, 1, jnp.int32) + jnp.max(pos, axis=1, keepdims=True)
    pick = pick_matrix(pos, base)
    for e in range(ne):
        fetch_w[e].wait()
        give_ref[0, e] = jnp.dot(pick, w_all[e], preferred_element_type=F32).astype(BF)


def keep_kernel(window, pos_ref, t_ref, w_ref, row_ref, keep_ref, t_all, w_all, sems):
    base = 0 if window is None else window[0] * CAP
    ne = keep_ref.shape[1]
    core = lax.axis_index("tr") % 2
    fetch_w = [pltpu.make_async_copy(w_ref.at[2 * e + core], w_all.at[e], sems.at[e]) for e in range(ne)]
    fetch_t = pltpu.make_async_copy(t_ref, t_all, sems.at[ne])
    for copy in fetch_w:
        copy.start()
    fetch_t.start()
    pick = pick_matrix(pos_ref[...], base)
    none = jnp.zeros_like(pick)
    for e in range(ne):
        fetch_w[e].wait()
        keep_ref[0, e] = jnp.dot(pick, w_all[e], preferred_element_type=F32).astype(BF)
    fetch_t.wait()
    ni, na, v = t_all.shape
    half = ni // 2
    low = t_all[:half].reshape(half * na, v)
    high = t_all[half:].reshape(half * na, v)
    dims = (((1,), (1,)), ((), ()))
    both = lax.dot_general(low, jnp.concatenate([pick, none], 0), dims, preferred_element_type=F32)
    both += lax.dot_general(high, jnp.concatenate([none, pick], 0), dims, preferred_element_type=F32)
    row_ref[0] = both.astype(BF).reshape(half, na, 2 * CAP)


def prepare_kernel(
    occ_ref, labels_ref, pos_ref, bits_ref, pick_own_ref, pick_other_ref, half_ref, spread_ref, expand_ref
):
    na, v = bits_ref.shape
    labels = labels_ref[...].reshape(1, v)
    pos = pos_ref[...]
    tr = lax.axis_index("tr")
    place = lax.broadcasted_iota(jnp.int32, (na, v), 0) + lax.axis_index("su") * na
    here = lax.broadcasted_iota(jnp.int32, (na, v), 1) == place
    labels_a = jnp.sum(jnp.where(here, labels, 0).astype(F32), axis=1, keepdims=True).astype(jnp.int32)
    plane = jnp.bitwise_xor(jnp.bitwise_xor(labels_a, labels), occ_ref[tr])
    bits = jnp.zeros((na, v), jnp.int32)
    for i in range(IW):
        bits += jnp.where(plane == occ_ref[i], 1 << i, 0)
    bits_ref[...] = bits
    rows_a = jnp.broadcast_to(labels_a, pick_own_ref.shape[1:])
    for i in range(IW):
        for ref, j in ((pick_own_ref, tr), (pick_other_ref, jnp.bitwise_xor(tr, 1))):
            ref[i] = jnp.right_shift(jnp.bitwise_xor(rows_a, jnp.bitwise_xor(occ_ref[i], occ_ref[j])), 1)
    upper = lax.broadcasted_iota(jnp.int32, rows_a.shape, 1) // CAP
    for i in range(IW):
        irrep = jnp.bitwise_xor(rows_a, jnp.bitwise_xor(occ_ref[i], occ_ref[tr]))
        half_ref[i] = (jnp.bitwise_and(irrep, 1) == upper).astype(jnp.int32)
    wide = lax.broadcasted_iota(jnp.int32, spread_ref.shape, 0) == labels * CAP + pos
    spread_ref[...] = wide.astype(F32).astype(BF)
    pair = lax.broadcasted_iota(jnp.int32, expand_ref.shape, 0) == jnp.bitwise_and(labels, 1) * CAP + pos
    expand_ref[...] = pair.astype(F32).astype(BF)


SMEM = pl.BlockSpec(memory_space=pltpu.SMEM)
VMEM = pl.BlockSpec(memory_space=pltpu.VMEM)
ANY = pl.BlockSpec(memory_space=pl.ANY)


def windowed(kernel, window):
    if window is None:
        return functools.partial(kernel, None), [], []
    return kernel, [SMEM], [window]


def pack_give(window, labels, w):
    nk, v, _ = w.shape
    kernel, specs, args = windowed(give_kernel, window)
    return pl.pallas_call(
        kernel,
        out_shape=(
            jax.ShapeDtypeStruct((1, nk // 2, CAP, v), BF),
            jax.ShapeDtypeStruct((1, v), jnp.int32),
            jax.ShapeDtypeStruct((1, 128), jnp.int32),
        ),
        in_specs=specs + [ANY, ANY],
        out_specs=(VMEM, VMEM, VMEM),
        scratch_shapes=[
            pltpu.VMEM((v,), jnp.int32),
            pltpu.VMEM((nk // 2, v, v), BF),
            pltpu.SemaphoreType.DMA((nk // 2 + 1,)),
        ],
        compiler_params=pltpu.CompilerParams(vmem_limit_bytes=8 * 2**20),
        name="pack_give",
    )(*args, labels, w)


def pack_keep(window, pos, t, w):
    nk, v, _ = w.shape
    ni, na, _ = t.shape
    kernel, specs, args = windowed(keep_kernel, window)
    return pl.pallas_call(
        kernel,
        out_shape=(
            jax.ShapeDtypeStruct((1, ni // 2, na, 2 * CAP), BF),
            jax.ShapeDtypeStruct((1, nk // 2, CAP, v), BF),
        ),
        in_specs=specs + [VMEM, ANY, ANY],
        out_specs=(VMEM, VMEM),
        scratch_shapes=[
            pltpu.VMEM(t.shape, BF),
            pltpu.VMEM((nk // 2, v, v), BF),
            pltpu.SemaphoreType.DMA((nk // 2 + 1,)),
        ],
        compiler_params=pltpu.CompilerParams(vmem_limit_bytes=8 * 2**20),
        cost_estimate=pl.CostEstimate(flops=0, bytes_accessed=4 * 2**20, transcendentals=0),
        name="pack_keep",
    )(*args, pos, t, w)


def prepare(occupied, labels, pos, na):
    v = labels.shape[0]
    pick = jax.ShapeDtypeStruct((IW, na, 2 * CAP), jnp.int32)
    return pl.pallas_call(
        prepare_kernel,
        out_shape=(
            jax.ShapeDtypeStruct((na, v), jnp.int32),
            pick,
            pick,
            pick,
            jax.ShapeDtypeStruct((8 * CAP, v), BF),
            jax.ShapeDtypeStruct((2 * CAP, v), BF),
        ),
        in_specs=[SMEM, VMEM, VMEM],
        out_specs=(VMEM,) * 6,
        compiler_params=pltpu.CompilerParams(vmem_limit_bytes=8 * 2**20),
        name="prepare",
    )(occupied, labels, pos)


OFFSETS = (0, 1, -1, 2, -2, 3, -3, 4)


def join_kernel(*refs):
    out_ref = refs[-1]
    at = 0
    for ref in refs[:-1]:
        out_ref[at : at + ref.shape[0]] = ref[...]
        at += ref.shape[0]


def join(name, *parts):
    shape = (sum(p.shape[0] for p in parts), *parts[0].shape[1:])
    size = 2 * 4 * math.prod(shape)
    return pl.pallas_call(
        join_kernel,
        out_shape=jax.ShapeDtypeStruct(shape, parts[0].dtype),
        in_specs=[VMEM] * len(parts),
        out_specs=VMEM,
        compiler_params=pltpu.CompilerParams(vmem_limit_bytes=8 * 2**20),
        cost_estimate=pl.CostEstimate(flops=0, bytes_accessed=size, transcendentals=0),
        name=name,
    )(*parts)


def lines(piece, first):
    return [lax.ppermute(piece, "tr", line(first, flip)) for flip in (1, 2, 3)]


def gather(keep, got, t, beside=lambda parts: ()):
    rows = lines(t, True)
    d = join("join_w", keep, got)
    a1 = lax.ppermute(d, "su", ODD_LINKS)
    b1 = lax.ppermute(d, "su", EVEN_LINKS)
    row = join("join_row", t, *rows)
    planes = lines(row, False)
    a2 = lax.ppermute(b1, "su", ODD_LINKS)
    b2 = lax.ppermute(a1, "su", EVEN_LINKS)
    a3 = lax.ppermute(b2, "su", ODD_LINKS)
    b3 = lax.ppermute(a2, "su", EVEN_LINKS)
    extra, a3 = lax.optimization_barrier((beside([d, a1, b1, a2, b2]), a3))
    a4 = lax.ppermute(b3[:1], "su", ODD_LINKS)
    b4 = lax.ppermute(a3[1:], "su", EVEN_LINKS)
    return [row, *planes], [d, a1, b1, a2, b2, a3, b3], a4, b4, extra


def blocks(d_refs, j, d_cat):
    _, ne, cap, v = d_refs[0].shape
    wide = ne * cap
    for n, d_ref in enumerate(d_refs):
        d_cat[n * wide : (n + 1) * wide] = d_ref[j].reshape(wide, v)


def other_kernel(*refs):
    t_refs, d_refs, (other_ref, t_cat, rest_ref, t_all, d_cat, sems) = refs[:4], refs[4:-6], refs[-6:]
    copies = [pltpu.make_async_copy(t_ref, t_all.at[NX * n : NX * n + NX], sems.at[n]) for n, t_ref in enumerate(t_refs)]
    for copy in copies:
        copy.start()
    _, ne, cap, v = d_refs[0].shape
    half_i, na = t_all.shape[1:3]
    rows = half_i * na
    wide = ne * cap
    blocks(d_refs, 1, d_cat)
    tr = lax.axis_index("tr")
    z = lax.axis_index("su")
    x, y, core = tr // (2 * NY), (tr // 2) % NY, tr % 2
    way = 1 - 2 * (z % 2)
    for copy in copies:
        copy.wait()
    for n, off in enumerate(OFFSETS):
        block = (z - off * way + NZ) % NZ
        pair = []
        for e in range(ne):
            chip = block * ne + e
            dx = jnp.bitwise_xor(chip // NY, x)
            dy = jnp.bitwise_xor(chip % NY, y)
            at = jnp.where(core == 0, dy * NX + dx, dx * NY + dy)
            pair.append(t_all[at].reshape(rows, 2 * CAP))
        for h in range(2):
            lanes = slice(h * CAP, (h + 1) * CAP)
            both = jnp.concatenate([pair[0][:, lanes], pair[1][:, lanes]], 1)
            if n < len(d_refs):
                t_cat[h, :, n * wide : (n + 1) * wide] = both
            else:
                rest_ref[h] = both
    for h in range(2):
        other_ref[h] = jnp.dot(t_cat[h], d_cat[...], preferred_element_type=F32)


def other_part(t_parts, d_parts):
    chips, half_i, na, lanes = t_parts[0].shape
    _, ne, cap, v = d_parts[0].shape
    rows = half_i * na
    wide = ne * cap
    depth = len(d_parts) * wide
    return pl.pallas_call(
        other_kernel,
        out_shape=(
            jax.ShapeDtypeStruct((2, rows, v), F32),
            jax.ShapeDtypeStruct((2, rows, depth), BF),
            jax.ShapeDtypeStruct((2, rows, wide), BF),
        ),
        in_specs=[ANY] * len(t_parts) + [VMEM] * len(d_parts),
        out_specs=(VMEM, VMEM, VMEM),
        scratch_shapes=[
            pltpu.VMEM((len(t_parts) * chips, half_i, na, lanes), BF),
            pltpu.VMEM((depth, v), BF),
            pltpu.SemaphoreType.DMA((len(t_parts),)),
        ],
        compiler_params=pltpu.CompilerParams(vmem_limit_bytes=20 * 2**20),
        cost_estimate=pl.CostEstimate(flops=4 * rows * v * depth, bytes_accessed=6 * 2**20, transcendentals=0),
        name="other_part",
    )(*t_parts, *d_parts)


def own_kernel(t_cat, *refs):
    d_refs, (own_ref, d_cat) = refs[:-2], refs[-2:]
    blocks(d_refs, 0, d_cat)
    for h in range(2):
        own_ref[h] = jnp.dot(t_cat[h], d_cat[...], preferred_element_type=F32)


def own_part(t_cat, d_parts):
    _, rows, depth = t_cat.shape
    v = d_parts[0].shape[3]
    return pl.pallas_call(
        own_kernel,
        out_shape=jax.ShapeDtypeStruct((2, rows, v), F32),
        in_specs=[VMEM] * (1 + len(d_parts)),
        out_specs=VMEM,
        scratch_shapes=[pltpu.VMEM((depth, v), BF)],
        compiler_params=pltpu.CompilerParams(vmem_limit_bytes=12 * 2**20),
        cost_estimate=pl.CostEstimate(flops=4 * rows * v * depth, bytes_accessed=4 * 2**20, transcendentals=0),
        name="own_part",
    )(t_cat, *d_parts)


def far_sum(h, sums_ref, rest_ref, d_ref):
    _, ne, cap, v = d_ref.shape
    return sums_ref[h] + jnp.dot(rest_ref[h], d_ref[0].reshape(ne * cap, v), preferred_element_type=F32)


def far_kernel(sums_ref, rest_ref, d_ref, out_ref):
    for h in range(2):
        out_ref[h] = far_sum(h, sums_ref, rest_ref, d_ref)


def far_part(sums, rest, d):
    return pl.pallas_call(
        far_kernel,
        out_shape=jax.ShapeDtypeStruct(sums.shape, F32),
        in_specs=[VMEM] * 3,
        out_specs=VMEM,
        compiler_params=pltpu.CompilerParams(vmem_limit_bytes=8 * 2**20),
        name="far_part",
    )(sums, rest, d)


def spread_kernel(spread_ref, *refs):
    d_refs, (own_ref, other_ref, d_cat) = refs[:-3], refs[-3:]
    dims = (((1,), (1,)), ((), ()))
    for j, ref in enumerate((own_ref, other_ref)):
        blocks(d_refs, j, d_cat)
        wide = lax.dot_general(d_cat[...], spread_ref[...], dims, preferred_element_type=F32)
        ref[...] = wide.astype(BF).reshape(ref.shape)


def spread_blocks(spread, d_parts):
    _, ne, cap, v = d_parts[0].shape
    count = len(d_parts) * ne
    out = jax.ShapeDtypeStruct((count, cap, spread.shape[0]), BF)
    return pl.pallas_call(
        spread_kernel,
        out_shape=(out, out),
        in_specs=[VMEM] * (1 + len(d_parts)),
        out_specs=(VMEM, VMEM),
        scratch_shapes=[pltpu.VMEM((count * cap, v), BF)],
        compiler_params=pltpu.CompilerParams(vmem_limit_bytes=8 * 2**20),
        cost_estimate=pl.CostEstimate(
            flops=4 * count * cap * v * spread.shape[0], bytes_accessed=4 * 2**20, transcendentals=0
        ),
        name="spread",
    )(spread, *d_parts)


def put_block(d_early, d_late, first, second, d_cat, at):
    src = block_at(first, second)
    early, late = d_early.shape[0], d_late.shape[0]
    near = d_early[jnp.minimum(src, early - 1)]
    far = d_late[jnp.clip(src - early, 0, late - 1)]
    far = jnp.where(src < early + late, far, jnp.zeros_like(far))
    d_cat[at : at + CAP] = jnp.where(src < early, near, far)


def block_at(first, second):
    tr = lax.axis_index("tr")
    z = lax.axis_index("su")
    x, y, core = tr // (2 * NY), (tr // 2) % NY, tr % 2
    to_x = jnp.bitwise_xor(x, jnp.where(core == 0, first, second))
    to_y = jnp.bitwise_xor(y, jnp.where(core == 0, second, first))
    ahead = (z - (2 * to_x + to_y // 2)) * (1 - 2 * (z % 2))
    hops = (ahead + 2 * NZ) % NZ
    arrival = jnp.where(hops == 0, 0, jnp.where(hops <= NZ // 2, 2 * hops - 1, 2 * (NZ - hops)))
    return 2 * arrival + to_y % 2


def pair_lanes(one, two, h):
    lanes = slice(h * CAP, (h + 1) * CAP)
    return jnp.concatenate([one[:, lanes], two[:, lanes]], 1)


def flat(piece):
    return piece.reshape(piece.shape[0] * piece.shape[1], piece.shape[2])


def early_kernel(*refs):
    t_refs, (d_early, d_late, other_ref, t_cat, d_cat) = refs[:-5], refs[-5:]
    lanes = 2 * CAP
    for second, t_ref in enumerate(t_refs):
        for p in range(NX // 2):
            one, two = flat(t_ref[2 * p]), flat(t_ref[2 * p + 1])
            at = (second * (NX // 2) + p) * lanes
            for h in range(2):
                t_cat[h, :, at : at + lanes] = pair_lanes(one, two, h)
            for u in range(2):
                put_block(d_early, d_late, 2 * p + u, second, d_cat, at + u * CAP)
    for h in range(2):
        other_ref[h] = jnp.dot(t_cat[h], d_cat[...], preferred_element_type=F32)


def early_sums(t_parts, d_other):
    chips, half_i, na, lanes = t_parts[0].shape
    rows = half_i * na
    depth = len(t_parts) * chips * CAP
    wide = d_other[0].shape[2]
    return pl.pallas_call(
        early_kernel,
        out_shape=(jax.ShapeDtypeStruct((2, rows, wide), F32), jax.ShapeDtypeStruct((2, rows, depth), BF)),
        in_specs=[VMEM] * (len(t_parts) + 2),
        out_specs=(VMEM, VMEM),
        scratch_shapes=[pltpu.VMEM((depth, wide), BF)],
        compiler_params=pltpu.CompilerParams(vmem_limit_bytes=16 * 2**20),
        cost_estimate=pl.CostEstimate(flops=4 * rows * wide * depth, bytes_accessed=6 * 2**20, transcendentals=0),
        name="early_sums",
    )(*t_parts, *d_other)


def keep_pair(sums, pick):
    lanes = 2 * CAP
    out = sums[:, :lanes]
    for g in range(1, 4):
        out = jnp.where(pick == g, sums[:, g * lanes : (g + 1) * lanes], out)
    return out


def other_pair_kernel(pick_ref, *refs):
    t_refs, (sums_ref, d_early, d_late, other_ref, late_ref, rest_ref, d_cat) = refs[:NX], refs[NX:]
    last = t_refs[-1]
    lanes = 2 * CAP
    for p in range(NX // 2):
        one, two = flat(last[2 * p]), flat(last[2 * p + 1])
        for h in range(2):
            late_ref[h, :, p * lanes : (p + 1) * lanes] = pair_lanes(one, two, h)
    for first in range(NX):
        put_block(d_early, d_late, first, NX - 1, d_cat, first * CAP)
    ni, na = other_ref.shape[:2]
    half_i = ni // 2
    for h in range(2):
        sums = sums_ref[h] + jnp.dot(late_ref[h], d_cat[...], preferred_element_type=F32)
        for u in range(half_i):
            i = h * half_i + u
            other_ref[i] = keep_pair(sums[u * na : (u + 1) * na], pick_ref[i])
    tr = lax.axis_index("tr")
    far = (lax.axis_index("su") + NZ // 2) % NZ
    x, y, core = tr // (2 * NY), (tr // 2) % NY, tr % 2
    pair = []
    for e in range(2):
        dx = jnp.bitwise_xor(far // 2, x)
        dy = jnp.bitwise_xor(2 * (far % 2) + e, y)
        first = jnp.where(core == 0, dx, dy)
        second = jnp.where(core == 0, dy, dx)
        piece = t_refs[0][first]
        for n in range(1, NX):
            piece = jnp.where(second == n, t_refs[n][first], piece)
        pair.append(flat(piece))
    for h in range(2):
        rest_ref[h] = pair_lanes(*pair, h)


def other_pair(pick, t_parts, sums, d):
    chips, half_i, na, lanes = t_parts[0].shape
    rows = half_i * na
    return pl.pallas_call(
        other_pair_kernel,
        out_shape=(
            jax.ShapeDtypeStruct(pick.shape, F32),
            jax.ShapeDtypeStruct((2, rows, chips * CAP), BF),
            jax.ShapeDtypeStruct((2, rows, lanes), BF),
        ),
        in_specs=[VMEM] * (4 + len(t_parts)),
        out_specs=(VMEM, VMEM, VMEM),
        scratch_shapes=[pltpu.VMEM((chips * CAP, sums.shape[2]), BF)],
        compiler_params=pltpu.CompilerParams(vmem_limit_bytes=12 * 2**20),
        cost_estimate=pl.CostEstimate(
            flops=4 * rows * sums.shape[2] * chips * CAP, bytes_accessed=6 * 2**20, transcendentals=0
        ),
        name="other_pair",
    )(pick, *t_parts, sums, *d)


def spread_far(d_ref, spread_ref):
    _, ne, cap, v = d_ref.shape
    dims = (((1,), (1,)), ((), ()))
    wide = lax.dot_general(d_ref[0].reshape(ne * cap, v), spread_ref[...], dims, preferred_element_type=F32)
    return wide.astype(BF)


def far_pair_kernel(pick_ref, spread_ref, sums_ref, rest_ref, d_ref, out_ref):
    right = spread_far(d_ref, spread_ref)
    ni, na = out_ref.shape[:2]
    half_i = ni // 2
    for h in range(2):
        sums = jnp.dot(rest_ref[h], right, preferred_element_type=F32)
        for u in range(half_i):
            i = h * half_i + u
            out_ref[i] = sums_ref[i] + keep_pair(sums[u * na : (u + 1) * na], pick_ref[i])


def far_pair(pick, spread, sums, rest, d):
    return pl.pallas_call(
        far_pair_kernel,
        out_shape=jax.ShapeDtypeStruct(pick.shape, F32),
        in_specs=[VMEM] * 5,
        out_specs=VMEM,
        compiler_params=pltpu.CompilerParams(vmem_limit_bytes=8 * 2**20),
        name="far_pair",
    )(pick, spread, sums, rest, d)


def own_pair_kernel(
    pick_ref, spread_ref, t_cat, late_ref, d_early, d_late, rest_ref, far_ref, own_ref, left_cat, d_cat
):
    at = 0
    for ref in (t_cat, late_ref, rest_ref):
        left_cat[:, :, at : at + ref.shape[2]] = ref[...]
        at += ref.shape[2]
    for second in range(NX):
        for first in range(NX):
            put_block(d_early, d_late, first, second, d_cat, (second * NX + first) * CAP)
    d_cat[NX * NX * CAP :] = spread_far(far_ref, spread_ref)
    ni, na = own_ref.shape[:2]
    half_i = ni // 2
    for h in range(2):
        sums = jnp.dot(left_cat[h], d_cat[...], preferred_element_type=F32)
        for u in range(half_i):
            i = h * half_i + u
            own_ref[i] = keep_pair(sums[u * na : (u + 1) * na], pick_ref[i])


def own_pair(pick, spread, t_cat, late, d, rest, far):
    rows = late.shape[1]
    depth = t_cat.shape[2] + late.shape[2] + rest.shape[2]
    wide = d[0].shape[2]
    return pl.pallas_call(
        own_pair_kernel,
        out_shape=jax.ShapeDtypeStruct(pick.shape, F32),
        in_specs=[VMEM] * 8,
        out_specs=VMEM,
        scratch_shapes=[pltpu.VMEM((2, rows, depth), BF), pltpu.VMEM((depth, wide), BF)],
        compiler_params=pltpu.CompilerParams(vmem_limit_bytes=12 * 2**20),
        cost_estimate=pl.CostEstimate(flops=4 * rows * wide * depth, bytes_accessed=4 * 2**20, transcendentals=0),
        name="own_pair",
    )(pick, spread, t_cat, late, *d, rest, far)


def last_kernel(width_ref, bits_ref, half_ref, expand_ref, own_ref, got_ref, out_ref, fits_ref):
    fits_ref[0] = (width_ref[0, 0] <= CAP).astype(jnp.int32)
    ni, na, lanes = own_ref.shape
    sums = jnp.where(half_ref[...] != 0, own_ref[...] + got_ref[...], 0.0)
    sums = sums.astype(BF).reshape(ni * na, lanes)
    wide = jnp.dot(sums, expand_ref[...], preferred_element_type=F32)
    for i in range(ni):
        keep = jnp.bitwise_and(bits_ref[...], 1 << i) != 0
        out_ref[i] = jnp.where(keep, wide[i * na : (i + 1) * na], 0.0).astype(BF)


def window_kernel(before_ref, own_ref, got_ref, rest_ref, d_ref, out_ref):
    for h in range(2):
        out_ref[h] = before_ref[h] + far_sum(h, own_ref, rest_ref, d_ref) + got_ref[h]


def body(amplitudes, integrals, occupied_irreps, virtual_irreps):
    ni, _, na, v = amplitudes.shape
    t = amplitudes.reshape(ni, na, v)
    w = integrals.reshape(integrals.shape[0], v, v)

    def pack(window):
        give, pos, width = pack_give(window, virtual_irreps, w)
        got = lax.ppermute(give, "tr", SWAP)
        row, keep = pack_keep(window, pos, t, w)
        return keep, got, row, pos, width

    keep, got, row, pos, width = pack(None)
    bits, pick_own, pick_other, half, spread, expand = prepare(occupied_irreps, virtual_irreps, pos, na)
    t_parts, d_parts, a4, b4, d_two = gather(keep, got, row, functools.partial(spread_blocks, spread))
    d_three = spread_blocks(spread, d_parts[5:])
    d_own, d_other = zip(d_two, d_three)
    sums_other, t_cat = early_sums(t_parts[:-1], d_other)
    other, t_late, rest = other_pair(pick_other, t_parts, sums_other, d_other)
    other, a4, b4 = lax.optimization_barrier((other, a4, b4))
    got = lax.ppermute(far_pair(pick_other, spread, other, rest, b4), "tr", SWAP)
    own = own_pair(pick_own, spread, t_cat, t_late, d_own, rest, a4)
    fast, fits = pl.pallas_call(
        last_kernel,
        out_shape=(jax.ShapeDtypeStruct((ni, na, v), BF), jax.ShapeDtypeStruct((1,), jnp.int32)),
        in_specs=[VMEM] * 6,
        out_specs=(VMEM, SMEM),
        compiler_params=pltpu.CompilerParams(vmem_limit_bytes=8 * 2**20),
        name="last_part",
    )(width, bits, half, expand, own, got)

    def all_windows():
        def window(n, before):
            keep, got, row, _, _ = pack(jnp.full((1,), n, jnp.int32))
            t_parts, d_parts, a4, b4, _ = gather(keep, got, row)
            other, t_cat, rest = other_part(t_parts, d_parts)
            got = lax.ppermute(far_part(other, rest, b4), "tr", SWAP)
            parts = (own_part(t_cat, d_parts), got, rest, a4)
            return pl.pallas_call(
                window_kernel,
                out_shape=jax.ShapeDtypeStruct(before.shape, F32),
                in_specs=[VMEM] * (1 + len(parts)),
                out_specs=VMEM,
                compiler_params=pltpu.CompilerParams(vmem_limit_bytes=16 * 2**20),
                name="window_part",
            )(before, *parts)

        windows = (width[0, 0] + CAP - 1) // CAP
        sums = lax.fori_loop(0, windows, window, jnp.zeros((2, ni // 2 * na, v), F32))
        label_j = occupied_irreps[lax.axis_index("tr")]
        labels_a = lax.dynamic_slice_in_dim(virtual_irreps, lax.axis_index("su") * na, na, 0)
        parity = jnp.bitwise_xor(occupied_irreps[:ni, None, None], label_j)
        parity = jnp.bitwise_xor(parity, labels_a[None, :, None])
        keep = jnp.bitwise_xor(parity, virtual_irreps[None, None, :]) == 0
        return jnp.where(keep, sums.reshape(ni, na, v).astype(BF), jnp.zeros((), BF))

    out = lax.cond(fits[0] == 1, lambda: fast, all_windows)
    return out.reshape(ni, 1, na, v)


def solution(mesh):
    return jax.shard_map(
        body,
        mesh=mesh,
        in_specs=(P(None, "tr", "su", None), P("su", None, "tr", None), P(), P()),
        out_specs=P(None, "tr", "su", None),
        check_vma=False,
    )
```

```python
import functools
import math

import jax
import jax.numpy as jnp
from jax import lax
from jax.experimental import pallas as pl
from jax.experimental.pallas import tpu as pltpu
from jax.sharding import PartitionSpec as P

BF = jnp.bfloat16
F32 = jnp.float32
IW = 16
CAP = 64
NX = NY = 4
NZ = 8


ODD_LINKS = [(z, (z + 1) % NZ if z % 2 else (z - 1) % NZ) for z in range(NZ)]
EVEN_LINKS = [(z, (z - 1) % NZ if z % 2 else (z + 1) % NZ) for z in range(NZ)]


def line(first, flip):
    pairs = []
    for x in range(NX):
        for y in range(NY):
            for c in range(2):
                along_x = (c == 0) == first
                to_x = x ^ flip if along_x else x
                to_y = y if along_x else y ^ flip
                pairs.append(((x * NY + y) * 2 + c, (to_x * NY + to_y) * 2 + c))
    return pairs


SWAP = [(d, d ^ 1) for d in range(2 * NX * NY)]


def pick_matrix(pos, base):
    rows = lax.broadcasted_iota(jnp.int32, (CAP, pos.shape[1]), 0) + base
    return (rows == pos).astype(F32).astype(BF)


def group_positions(labels):
    pos = lax.broadcasted_iota(jnp.int32, labels.shape, 1)
    for g in range(1, 8):
        first = jnp.sum((labels < g).astype(F32), axis=1, keepdims=True).astype(jnp.int32)
        pos -= jnp.where(labels == g, first, 0)
    return pos


def give_kernel(window, labels_ref, t_ref, w_ref, give_ref, pos_ref, width_ref, t_all, w_keep, l_all, w_all, sems):
    base = 0 if window is None else window[0] * CAP
    ne = give_ref.shape[1]
    core = lax.axis_index("tr") % 2
    fetch_l = pltpu.make_async_copy(labels_ref, l_all, sems.at[0])
    fetch_w = [pltpu.make_async_copy(w_ref.at[2 * e + 1 - core], w_all.at[e], sems.at[1 + e]) for e in range(ne)]
    later = [pltpu.make_async_copy(w_ref.at[2 * e + core], w_keep.at[e], sems.at[1 + ne + e]) for e in range(ne)]
    later.append(pltpu.make_async_copy(t_ref, t_all, sems.at[1 + 2 * ne]))
    fetch_l.start()
    for copy in fetch_w + later:
        copy.start()
    fetch_l.wait()
    pos = group_positions(l_all[...].reshape(1, l_all.shape[0]))
    pos_ref[...] = pos
    width_ref[...] = jnp.full(width_ref.shape, 1, jnp.int32) + jnp.max(pos, axis=1, keepdims=True)
    pick = pick_matrix(pos, base)
    for e in range(ne):
        fetch_w[e].wait()
        give_ref[0, e] = jnp.dot(pick, w_all[e], preferred_element_type=F32).astype(BF)
    for copy in later:
        copy.wait()


def keep_kernel(window, pos_ref, t_ref, w_ref, row_ref, keep_ref):
    base = 0 if window is None else window[0] * CAP
    pick = pick_matrix(pos_ref[...], base)
    none = jnp.zeros_like(pick)
    for e in range(keep_ref.shape[1]):
        keep_ref[0, e] = jnp.dot(pick, w_ref[e], preferred_element_type=F32).astype(BF)
    ni, na, v = t_ref.shape
    half = ni // 2
    low = t_ref[:half].reshape(half * na, v)
    high = t_ref[half:].reshape(half * na, v)
    dims = (((1,), (1,)), ((), ()))
    both = lax.dot_general(low, jnp.concatenate([pick, none], 0), dims, preferred_element_type=F32)
    both += lax.dot_general(high, jnp.concatenate([none, pick], 0), dims, preferred_element_type=F32)
    row_ref[0] = both.astype(BF).reshape(half, na, 2 * CAP)


def prepare_kernel(
    occ_ref, labels_ref, pos_ref, bits_ref, pick_own_ref, pick_other_ref, half_ref, spread_ref, expand_ref
):
    na, v = bits_ref.shape
    labels = labels_ref[...].reshape(1, v)
    pos = pos_ref[...]
    tr = lax.axis_index("tr")
    place = lax.broadcasted_iota(jnp.int32, (na, v), 0) + lax.axis_index("su") * na
    here = lax.broadcasted_iota(jnp.int32, (na, v), 1) == place
    labels_a = jnp.sum(jnp.where(here, labels, 0).astype(F32), axis=1, keepdims=True).astype(jnp.int32)
    plane = jnp.bitwise_xor(jnp.bitwise_xor(labels_a, labels), occ_ref[tr])
    bits = jnp.zeros((na, v), jnp.int32)
    for i in range(IW):
        bits += jnp.where(plane == occ_ref[i], 1 << i, 0)
    bits_ref[...] = bits
    rows_a = jnp.broadcast_to(labels_a, pick_own_ref.shape[1:])
    for i in range(IW):
        for ref, j in ((pick_own_ref, tr), (pick_other_ref, jnp.bitwise_xor(tr, 1))):
            ref[i] = jnp.right_shift(jnp.bitwise_xor(rows_a, jnp.bitwise_xor(occ_ref[i], occ_ref[j])), 1)
    upper = lax.broadcasted_iota(jnp.int32, rows_a.shape, 1) // CAP
    for i in range(IW):
        irrep = jnp.bitwise_xor(rows_a, jnp.bitwise_xor(occ_ref[i], occ_ref[tr]))
        half_ref[i] = (jnp.bitwise_and(irrep, 1) == upper).astype(jnp.int32)
    wide = lax.broadcasted_iota(jnp.int32, spread_ref.shape, 0) == labels * CAP + pos
    spread_ref[...] = wide.astype(F32).astype(BF)
    pair = lax.broadcasted_iota(jnp.int32, expand_ref.shape, 0) == jnp.bitwise_and(labels, 1) * CAP + pos
    expand_ref[...] = pair.astype(F32).astype(BF)


SMEM = pl.BlockSpec(memory_space=pltpu.SMEM)
VMEM = pl.BlockSpec(memory_space=pltpu.VMEM)
ANY = pl.BlockSpec(memory_space=pl.ANY)


def windowed(kernel, window):
    if window is None:
        return functools.partial(kernel, None), [], []
    return kernel, [SMEM], [window]


def pack_give(window, labels, t, w):
    nk, v, _ = w.shape
    kernel, specs, args = windowed(give_kernel, window)
    return pl.pallas_call(
        kernel,
        out_shape=(
            jax.ShapeDtypeStruct((1, nk // 2, CAP, v), BF),
            jax.ShapeDtypeStruct((1, v), jnp.int32),
            jax.ShapeDtypeStruct((1, 128), jnp.int32),
            jax.ShapeDtypeStruct(t.shape, BF),
            jax.ShapeDtypeStruct((nk // 2, v, v), BF),
        ),
        in_specs=specs + [ANY] * 3,
        out_specs=(VMEM,) * 5,
        scratch_shapes=[
            pltpu.VMEM((v,), jnp.int32),
            pltpu.VMEM((nk // 2, v, v), BF),
            pltpu.SemaphoreType.DMA((nk + 2,)),
        ],
        compiler_params=pltpu.CompilerParams(vmem_limit_bytes=8 * 2**20),
        name="pack_give",
    )(*args, labels, t, w)


def pack_keep(window, pos, t, w):
    nk, v, _ = w.shape
    ni, na, _ = t.shape
    kernel, specs, args = windowed(keep_kernel, window)
    return pl.pallas_call(
        kernel,
        out_shape=(
            jax.ShapeDtypeStruct((1, ni // 2, na, 2 * CAP), BF),
            jax.ShapeDtypeStruct((1, nk, CAP, v), BF),
        ),
        in_specs=specs + [VMEM] * 3,
        out_specs=(VMEM, VMEM),
        compiler_params=pltpu.CompilerParams(vmem_limit_bytes=8 * 2**20),
        cost_estimate=pl.CostEstimate(flops=0, bytes_accessed=4 * 2**20, transcendentals=0),
        name="pack_keep",
    )(*args, pos, t, w)


def prepare(occupied, labels, pos, na):
    v = labels.shape[0]
    pick = jax.ShapeDtypeStruct((IW, na, 2 * CAP), jnp.int32)
    return pl.pallas_call(
        prepare_kernel,
        out_shape=(
            jax.ShapeDtypeStruct((na, v), jnp.int32),
            pick,
            pick,
            pick,
            jax.ShapeDtypeStruct((8 * CAP, v), BF),
            jax.ShapeDtypeStruct((2 * CAP, v), BF),
        ),
        in_specs=[SMEM, VMEM, VMEM],
        out_specs=(VMEM,) * 6,
        compiler_params=pltpu.CompilerParams(vmem_limit_bytes=8 * 2**20),
        name="prepare",
    )(occupied, labels, pos)


OFFSETS = (0, 1, -1, 2, -2, 3, -3, 4)


def join_kernel(*refs):
    out_ref = refs[-1]
    at = 0
    for ref in refs[:-1]:
        out_ref[at : at + ref.shape[0]] = ref[...]
        at += ref.shape[0]


def join(name, *parts):
    shape = (sum(p.shape[0] for p in parts), *parts[0].shape[1:])
    size = 2 * 4 * math.prod(shape)
    return pl.pallas_call(
        join_kernel,
        out_shape=jax.ShapeDtypeStruct(shape, parts[0].dtype),
        in_specs=[VMEM] * len(parts),
        out_specs=VMEM,
        compiler_params=pltpu.CompilerParams(vmem_limit_bytes=8 * 2**20),
        cost_estimate=pl.CostEstimate(flops=0, bytes_accessed=size, transcendentals=0),
        name=name,
    )(*parts)


def lines(piece, first):
    return [lax.ppermute(piece, "tr", line(first, flip)) for flip in (1, 2, 3)]


def gather(keep, got, t, beside=lambda parts: ()):
    rows = lines(t, True)
    d = join("join_w", keep, got)
    a1 = lax.ppermute(d, "su", ODD_LINKS)
    b1 = lax.ppermute(d, "su", EVEN_LINKS)
    row = join("join_row", t, *rows)
    planes = lines(row, False)
    a2 = lax.ppermute(b1, "su", ODD_LINKS)
    b2 = lax.ppermute(a1, "su", EVEN_LINKS)
    a3 = lax.ppermute(b2, "su", ODD_LINKS)
    b3 = lax.ppermute(a2, "su", EVEN_LINKS)
    extra, a3 = lax.optimization_barrier((beside([d, a1, b1, a2, b2]), a3))
    a4 = lax.ppermute(b3[:1], "su", ODD_LINKS)
    b4 = lax.ppermute(a3[1:], "su", EVEN_LINKS)
    return [row, *planes], [d, a1, b1, a2, b2, a3, b3], a4, b4, extra


def blocks(d_refs, j, d_cat):
    _, ne, cap, v = d_refs[0].shape
    wide = ne * cap
    for n, d_ref in enumerate(d_refs):
        d_cat[n * wide : (n + 1) * wide] = d_ref[j].reshape(wide, v)


def other_kernel(*refs):
    t_refs, d_refs, (other_ref, t_cat, rest_ref, t_all, d_cat, sems) = refs[:4], refs[4:-6], refs[-6:]
    copies = [pltpu.make_async_copy(t_ref, t_all.at[NX * n : NX * n + NX], sems.at[n]) for n, t_ref in enumerate(t_refs)]
    for copy in copies:
        copy.start()
    _, ne, cap, v = d_refs[0].shape
    half_i, na = t_all.shape[1:3]
    rows = half_i * na
    wide = ne * cap
    blocks(d_refs, 1, d_cat)
    tr = lax.axis_index("tr")
    z = lax.axis_index("su")
    x, y, core = tr // (2 * NY), (tr // 2) % NY, tr % 2
    way = 1 - 2 * (z % 2)
    for copy in copies:
        copy.wait()
    for n, off in enumerate(OFFSETS):
        block = (z - off * way + NZ) % NZ
        pair = []
        for e in range(ne):
            chip = block * ne + e
            dx = jnp.bitwise_xor(chip // NY, x)
            dy = jnp.bitwise_xor(chip % NY, y)
            at = jnp.where(core == 0, dy * NX + dx, dx * NY + dy)
            pair.append(t_all[at].reshape(rows, 2 * CAP))
        for h in range(2):
            lanes = slice(h * CAP, (h + 1) * CAP)
            both = jnp.concatenate([pair[0][:, lanes], pair[1][:, lanes]], 1)
            if n < len(d_refs):
                t_cat[h, :, n * wide : (n + 1) * wide] = both
            else:
                rest_ref[h] = both
    for h in range(2):
        other_ref[h] = jnp.dot(t_cat[h], d_cat[...], preferred_element_type=F32)


def other_part(t_parts, d_parts):
    chips, half_i, na, lanes = t_parts[0].shape
    _, ne, cap, v = d_parts[0].shape
    rows = half_i * na
    wide = ne * cap
    depth = len(d_parts) * wide
    return pl.pallas_call(
        other_kernel,
        out_shape=(
            jax.ShapeDtypeStruct((2, rows, v), F32),
            jax.ShapeDtypeStruct((2, rows, depth), BF),
            jax.ShapeDtypeStruct((2, rows, wide), BF),
        ),
        in_specs=[ANY] * len(t_parts) + [VMEM] * len(d_parts),
        out_specs=(VMEM, VMEM, VMEM),
        scratch_shapes=[
            pltpu.VMEM((len(t_parts) * chips, half_i, na, lanes), BF),
            pltpu.VMEM((depth, v), BF),
            pltpu.SemaphoreType.DMA((len(t_parts),)),
        ],
        compiler_params=pltpu.CompilerParams(vmem_limit_bytes=20 * 2**20),
        cost_estimate=pl.CostEstimate(flops=4 * rows * v * depth, bytes_accessed=6 * 2**20, transcendentals=0),
        name="other_part",
    )(*t_parts, *d_parts)


def own_kernel(t_cat, *refs):
    d_refs, (own_ref, d_cat) = refs[:-2], refs[-2:]
    blocks(d_refs, 0, d_cat)
    for h in range(2):
        own_ref[h] = jnp.dot(t_cat[h], d_cat[...], preferred_element_type=F32)


def own_part(t_cat, d_parts):
    _, rows, depth = t_cat.shape
    v = d_parts[0].shape[3]
    return pl.pallas_call(
        own_kernel,
        out_shape=jax.ShapeDtypeStruct((2, rows, v), F32),
        in_specs=[VMEM] * (1 + len(d_parts)),
        out_specs=VMEM,
        scratch_shapes=[pltpu.VMEM((depth, v), BF)],
        compiler_params=pltpu.CompilerParams(vmem_limit_bytes=12 * 2**20),
        cost_estimate=pl.CostEstimate(flops=4 * rows * v * depth, bytes_accessed=4 * 2**20, transcendentals=0),
        name="own_part",
    )(t_cat, *d_parts)


def far_sum(h, sums_ref, rest_ref, d_ref):
    _, ne, cap, v = d_ref.shape
    return sums_ref[h] + jnp.dot(rest_ref[h], d_ref[0].reshape(ne * cap, v), preferred_element_type=F32)


def far_kernel(sums_ref, rest_ref, d_ref, out_ref):
    for h in range(2):
        out_ref[h] = far_sum(h, sums_ref, rest_ref, d_ref)


def far_part(sums, rest, d):
    return pl.pallas_call(
        far_kernel,
        out_shape=jax.ShapeDtypeStruct(sums.shape, F32),
        in_specs=[VMEM] * 3,
        out_specs=VMEM,
        compiler_params=pltpu.CompilerParams(vmem_limit_bytes=8 * 2**20),
        name="far_part",
    )(sums, rest, d)


def spread_kernel(spread_ref, *refs):
    d_refs, (own_ref, other_ref, d_cat) = refs[:-3], refs[-3:]
    dims = (((1,), (1,)), ((), ()))
    for j, ref in enumerate((own_ref, other_ref)):
        blocks(d_refs, j, d_cat)
        wide = lax.dot_general(d_cat[...], spread_ref[...], dims, preferred_element_type=F32)
        ref[...] = wide.astype(BF).reshape(ref.shape)


def spread_blocks(spread, d_parts):
    _, ne, cap, v = d_parts[0].shape
    count = len(d_parts) * ne
    out = jax.ShapeDtypeStruct((count, cap, spread.shape[0]), BF)
    return pl.pallas_call(
        spread_kernel,
        out_shape=(out, out),
        in_specs=[VMEM] * (1 + len(d_parts)),
        out_specs=(VMEM, VMEM),
        scratch_shapes=[pltpu.VMEM((count * cap, v), BF)],
        compiler_params=pltpu.CompilerParams(vmem_limit_bytes=8 * 2**20),
        cost_estimate=pl.CostEstimate(
            flops=4 * count * cap * v * spread.shape[0], bytes_accessed=4 * 2**20, transcendentals=0
        ),
        name="spread",
    )(spread, *d_parts)


def put_block(d_early, d_late, first, second, d_cat, at):
    src = block_at(first, second)
    early, late = d_early.shape[0], d_late.shape[0]
    near = d_early[jnp.minimum(src, early - 1)]
    far = d_late[jnp.clip(src - early, 0, late - 1)]
    far = jnp.where(src < early + late, far, jnp.zeros_like(far))
    d_cat[at : at + CAP] = jnp.where(src < early, near, far)


def block_at(first, second):
    tr = lax.axis_index("tr")
    z = lax.axis_index("su")
    x, y, core = tr // (2 * NY), (tr // 2) % NY, tr % 2
    to_x = jnp.bitwise_xor(x, jnp.where(core == 0, first, second))
    to_y = jnp.bitwise_xor(y, jnp.where(core == 0, second, first))
    ahead = (z - (2 * to_x + to_y // 2)) * (1 - 2 * (z % 2))
    hops = (ahead + 2 * NZ) % NZ
    arrival = jnp.where(hops == 0, 0, jnp.where(hops <= NZ // 2, 2 * hops - 1, 2 * (NZ - hops)))
    return 2 * arrival + to_y % 2


def pair_lanes(one, two, h):
    lanes = slice(h * CAP, (h + 1) * CAP)
    return jnp.concatenate([one[:, lanes], two[:, lanes]], 1)


def flat(piece):
    return piece.reshape(piece.shape[0] * piece.shape[1], piece.shape[2])


def early_kernel(*refs):
    t_refs, (d_early, d_late, other_ref, t_cat, d_cat) = refs[:-5], refs[-5:]
    lanes = 2 * CAP
    for second, t_ref in enumerate(t_refs):
        for p in range(NX // 2):
            one, two = flat(t_ref[2 * p]), flat(t_ref[2 * p + 1])
            at = (second * (NX // 2) + p) * lanes
            for h in range(2):
                t_cat[h, :, at : at + lanes] = pair_lanes(one, two, h)
            for u in range(2):
                put_block(d_early, d_late, 2 * p + u, second, d_cat, at + u * CAP)
    for h in range(2):
        other_ref[h] = jnp.dot(t_cat[h], d_cat[...], preferred_element_type=F32)


def early_sums(t_parts, d_other):
    chips, half_i, na, lanes = t_parts[0].shape
    rows = half_i * na
    depth = len(t_parts) * chips * CAP
    wide = d_other[0].shape[2]
    return pl.pallas_call(
        early_kernel,
        out_shape=(jax.ShapeDtypeStruct((2, rows, wide), F32), jax.ShapeDtypeStruct((2, rows, depth), BF)),
        in_specs=[VMEM] * (len(t_parts) + 2),
        out_specs=(VMEM, VMEM),
        scratch_shapes=[pltpu.VMEM((depth, wide), BF)],
        compiler_params=pltpu.CompilerParams(vmem_limit_bytes=16 * 2**20),
        cost_estimate=pl.CostEstimate(flops=4 * rows * wide * depth, bytes_accessed=6 * 2**20, transcendentals=0),
        name="early_sums",
    )(*t_parts, *d_other)


def keep_pair(sums, pick):
    lanes = 2 * CAP
    out = sums[:, :lanes]
    for g in range(1, 4):
        out = jnp.where(pick == g, sums[:, g * lanes : (g + 1) * lanes], out)
    return out


def other_pair_kernel(pick_ref, *refs):
    t_refs, (sums_ref, d_early, d_late, other_ref, late_ref, rest_ref, d_cat) = refs[:NX], refs[NX:]
    last = t_refs[-1]
    lanes = 2 * CAP
    for p in range(NX // 2):
        one, two = flat(last[2 * p]), flat(last[2 * p + 1])
        for h in range(2):
            late_ref[h, :, p * lanes : (p + 1) * lanes] = pair_lanes(one, two, h)
    for first in range(NX):
        put_block(d_early, d_late, first, NX - 1, d_cat, first * CAP)
    ni, na = other_ref.shape[:2]
    half_i = ni // 2
    for h in range(2):
        sums = sums_ref[h] + jnp.dot(late_ref[h], d_cat[...], preferred_element_type=F32)
        for u in range(half_i):
            i = h * half_i + u
            other_ref[i] = keep_pair(sums[u * na : (u + 1) * na], pick_ref[i])
    tr = lax.axis_index("tr")
    far = (lax.axis_index("su") + NZ // 2) % NZ
    x, y, core = tr // (2 * NY), (tr // 2) % NY, tr % 2
    pair = []
    for e in range(2):
        dx = jnp.bitwise_xor(far // 2, x)
        dy = jnp.bitwise_xor(2 * (far % 2) + e, y)
        first = jnp.where(core == 0, dx, dy)
        second = jnp.where(core == 0, dy, dx)
        piece = t_refs[0][first]
        for n in range(1, NX):
            piece = jnp.where(second == n, t_refs[n][first], piece)
        pair.append(flat(piece))
    for h in range(2):
        rest_ref[h] = pair_lanes(*pair, h)


def other_pair(pick, t_parts, sums, d):
    chips, half_i, na, lanes = t_parts[0].shape
    rows = half_i * na
    return pl.pallas_call(
        other_pair_kernel,
        out_shape=(
            jax.ShapeDtypeStruct(pick.shape, F32),
            jax.ShapeDtypeStruct((2, rows, chips * CAP), BF),
            jax.ShapeDtypeStruct((2, rows, lanes), BF),
        ),
        in_specs=[VMEM] * (4 + len(t_parts)),
        out_specs=(VMEM, VMEM, VMEM),
        scratch_shapes=[pltpu.VMEM((chips * CAP, sums.shape[2]), BF)],
        compiler_params=pltpu.CompilerParams(vmem_limit_bytes=12 * 2**20),
        cost_estimate=pl.CostEstimate(
            flops=4 * rows * sums.shape[2] * chips * CAP, bytes_accessed=6 * 2**20, transcendentals=0
        ),
        name="other_pair",
    )(pick, *t_parts, sums, *d)


def spread_far(d_ref, spread_ref):
    _, ne, cap, v = d_ref.shape
    dims = (((1,), (1,)), ((), ()))
    wide = lax.dot_general(d_ref[0].reshape(ne * cap, v), spread_ref[...], dims, preferred_element_type=F32)
    return wide.astype(BF)


def far_pair_kernel(pick_ref, spread_ref, sums_ref, rest_ref, d_ref, out_ref):
    right = spread_far(d_ref, spread_ref)
    ni, na = out_ref.shape[:2]
    half_i = ni // 2
    for h in range(2):
        sums = jnp.dot(rest_ref[h], right, preferred_element_type=F32)
        for u in range(half_i):
            i = h * half_i + u
            out_ref[i] = sums_ref[i] + keep_pair(sums[u * na : (u + 1) * na], pick_ref[i])


def far_pair(pick, spread, sums, rest, d):
    return pl.pallas_call(
        far_pair_kernel,
        out_shape=jax.ShapeDtypeStruct(pick.shape, F32),
        in_specs=[VMEM] * 5,
        out_specs=VMEM,
        compiler_params=pltpu.CompilerParams(vmem_limit_bytes=8 * 2**20),
        name="far_pair",
    )(pick, spread, sums, rest, d)


def own_pair_kernel(
    pick_ref, spread_ref, t_cat, late_ref, d_early, d_late, rest_ref, far_ref, own_ref, left_cat, d_cat
):
    at = 0
    for ref in (t_cat, late_ref, rest_ref):
        left_cat[:, :, at : at + ref.shape[2]] = ref[...]
        at += ref.shape[2]
    for second in range(NX):
        for first in range(NX):
            put_block(d_early, d_late, first, second, d_cat, (second * NX + first) * CAP)
    d_cat[NX * NX * CAP :] = spread_far(far_ref, spread_ref)
    ni, na = own_ref.shape[:2]
    half_i = ni // 2
    for h in range(2):
        sums = jnp.dot(left_cat[h], d_cat[...], preferred_element_type=F32)
        for u in range(half_i):
            i = h * half_i + u
            own_ref[i] = keep_pair(sums[u * na : (u + 1) * na], pick_ref[i])


def own_pair(pick, spread, t_cat, late, d, rest, far):
    rows = late.shape[1]
    depth = t_cat.shape[2] + late.shape[2] + rest.shape[2]
    wide = d[0].shape[2]
    return pl.pallas_call(
        own_pair_kernel,
        out_shape=jax.ShapeDtypeStruct(pick.shape, F32),
        in_specs=[VMEM] * 8,
        out_specs=VMEM,
        scratch_shapes=[pltpu.VMEM((2, rows, depth), BF), pltpu.VMEM((depth, wide), BF)],
        compiler_params=pltpu.CompilerParams(vmem_limit_bytes=12 * 2**20),
        cost_estimate=pl.CostEstimate(flops=4 * rows * wide * depth, bytes_accessed=4 * 2**20, transcendentals=0),
        name="own_pair",
    )(pick, spread, t_cat, late, *d, rest, far)


def last_kernel(width_ref, bits_ref, half_ref, expand_ref, own_ref, got_ref, out_ref, fits_ref):
    fits_ref[0] = (width_ref[0, 0] <= CAP).astype(jnp.int32)
    ni, na, lanes = own_ref.shape
    sums = jnp.where(half_ref[...] != 0, own_ref[...] + got_ref[...], 0.0)
    sums = sums.astype(BF).reshape(ni * na, lanes)
    wide = jnp.dot(sums, expand_ref[...], preferred_element_type=F32)
    for i in range(ni):
        keep = jnp.bitwise_and(bits_ref[...], 1 << i) != 0
        out_ref[i] = jnp.where(keep, wide[i * na : (i + 1) * na], 0.0).astype(BF)


def window_kernel(before_ref, own_ref, got_ref, rest_ref, d_ref, out_ref):
    for h in range(2):
        out_ref[h] = before_ref[h] + far_sum(h, own_ref, rest_ref, d_ref) + got_ref[h]


def body(amplitudes, integrals, occupied_irreps, virtual_irreps):
    ni, _, na, v = amplitudes.shape
    t = amplitudes.reshape(ni, na, v)
    w = integrals.reshape(integrals.shape[0], v, v)

    def pack(window):
        give, pos, width, t_here, w_here = pack_give(window, virtual_irreps, t, w)
        got = lax.ppermute(give, "tr", SWAP)
        row, keep = pack_keep(window, pos, t_here, w_here)
        return keep, got, row, pos, width

    keep, got, row, pos, width = pack(None)
    bits, pick_own, pick_other, half, spread, expand = prepare(occupied_irreps, virtual_irreps, pos, na)
    t_parts, d_parts, a4, b4, d_two = gather(keep, got, row, functools.partial(spread_blocks, spread))
    d_three = spread_blocks(spread, d_parts[5:])
    d_own, d_other = zip(d_two, d_three)
    sums_other, t_cat = early_sums(t_parts[:-1], d_other)
    other, t_late, rest = other_pair(pick_other, t_parts, sums_other, d_other)
    other, a4, b4 = lax.optimization_barrier((other, a4, b4))
    got = lax.ppermute(far_pair(pick_other, spread, other, rest, b4), "tr", SWAP)
    own = own_pair(pick_own, spread, t_cat, t_late, d_own, rest, a4)
    fast, fits = pl.pallas_call(
        last_kernel,
        out_shape=(jax.ShapeDtypeStruct((ni, na, v), BF), jax.ShapeDtypeStruct((1,), jnp.int32)),
        in_specs=[VMEM] * 6,
        out_specs=(VMEM, SMEM),
        compiler_params=pltpu.CompilerParams(vmem_limit_bytes=8 * 2**20),
        name="last_part",
    )(width, bits, half, expand, own, got)

    def all_windows():
        def window(n, before):
            keep, got, row, _, _ = pack(jnp.full((1,), n, jnp.int32))
            t_parts, d_parts, a4, b4, _ = gather(keep, got, row)
            other, t_cat, rest = other_part(t_parts, d_parts)
            got = lax.ppermute(far_part(other, rest, b4), "tr", SWAP)
            parts = (own_part(t_cat, d_parts), got, rest, a4)
            return pl.pallas_call(
                window_kernel,
                out_shape=jax.ShapeDtypeStruct(before.shape, F32),
                in_specs=[VMEM] * (1 + len(parts)),
                out_specs=VMEM,
                compiler_params=pltpu.CompilerParams(vmem_limit_bytes=16 * 2**20),
                name="window_part",
            )(before, *parts)

        windows = (width[0, 0] + CAP - 1) // CAP
        sums = lax.fori_loop(0, windows, window, jnp.zeros((2, ni // 2 * na, v), F32))
        label_j = occupied_irreps[lax.axis_index("tr")]
        labels_a = lax.dynamic_slice_in_dim(virtual_irreps, lax.axis_index("su") * na, na, 0)
        parity = jnp.bitwise_xor(occupied_irreps[:ni, None, None], label_j)
        parity = jnp.bitwise_xor(parity, labels_a[None, :, None])
        keep = jnp.bitwise_xor(parity, virtual_irreps[None, None, :]) == 0
        return jnp.where(keep, sums.reshape(ni, na, v).astype(BF), jnp.zeros((), BF))

    out = lax.cond(fits[0] == 1, lambda: fast, all_windows)
    return out.reshape(ni, 1, na, v)


def solution(mesh):
    return jax.shard_map(
        body,
        mesh=mesh,
        in_specs=(P(None, "tr", "su", None), P("su", None, "tr", None), P(), P()),
        out_specs=P(None, "tr", "su", None),
        check_vma=False,
    )
```

```python
import functools
import math

import jax
import jax.numpy as jnp
from jax import lax
from jax.experimental import pallas as pl
from jax.experimental.pallas import tpu as pltpu
from jax.sharding import PartitionSpec as P

BF = jnp.bfloat16
F32 = jnp.float32
IW = 16
CAP = 64
NX = NY = 4
NZ = 8


ODD_LINKS = [(z, (z + 1) % NZ if z % 2 else (z - 1) % NZ) for z in range(NZ)]
EVEN_LINKS = [(z, (z - 1) % NZ if z % 2 else (z + 1) % NZ) for z in range(NZ)]


def line(first, flip):
    pairs = []
    for x in range(NX):
        for y in range(NY):
            for c in range(2):
                along_x = (c == 0) == first
                to_x = x ^ flip if along_x else x
                to_y = y if along_x else y ^ flip
                pairs.append(((x * NY + y) * 2 + c, (to_x * NY + to_y) * 2 + c))
    return pairs


SWAP = [(d, d ^ 1) for d in range(2 * NX * NY)]


def pick_matrix(pos, base):
    rows = lax.broadcasted_iota(jnp.int32, (CAP, pos.shape[1]), 0) + base
    return (rows == pos).astype(F32).astype(BF)


def group_positions(labels):
    pos = lax.broadcasted_iota(jnp.int32, labels.shape, 1)
    for g in range(1, 8):
        first = jnp.sum((labels < g).astype(F32), axis=1, keepdims=True).astype(jnp.int32)
        pos -= jnp.where(labels == g, first, 0)
    return pos


def give_kernel(window, labels_ref, t_ref, w_ref, give_ref, pos_ref, width_ref, t_all, w_keep, l_all, w_all, sems):
    base = 0 if window is None else window[0] * CAP
    ne = give_ref.shape[1]
    core = lax.axis_index("tr") % 2
    fetch_l = pltpu.make_async_copy(labels_ref, l_all, sems.at[0])
    fetch_w = [pltpu.make_async_copy(w_ref.at[2 * e + 1 - core], w_all.at[e], sems.at[1 + e]) for e in range(ne)]
    later = [pltpu.make_async_copy(w_ref.at[2 * e + core], w_keep.at[e], sems.at[1 + ne + e]) for e in range(ne)]
    later.append(pltpu.make_async_copy(t_ref, t_all, sems.at[1 + 2 * ne]))
    fetch_l.start()
    for copy in fetch_w + later:
        copy.start()
    fetch_l.wait()
    pos = group_positions(l_all[...].reshape(1, l_all.shape[0]))
    pos_ref[...] = pos
    width_ref[...] = jnp.full(width_ref.shape, 1, jnp.int32) + jnp.max(pos, axis=1, keepdims=True)
    pick = pick_matrix(pos, base)
    for e in range(ne):
        fetch_w[e].wait()
        give_ref[0, e] = jnp.dot(pick, w_all[e], preferred_element_type=F32).astype(BF)
    for copy in later:
        copy.wait()


def keep_kernel(window, pos_ref, t_ref, w_ref, row_ref, keep_ref):
    base = 0 if window is None else window[0] * CAP
    pick = pick_matrix(pos_ref[...], base)
    none = jnp.zeros_like(pick)
    for e in range(keep_ref.shape[1]):
        keep_ref[0, e] = jnp.dot(pick, w_ref[e], preferred_element_type=F32).astype(BF)
    ni, na, v = t_ref.shape
    half = ni // 2
    low = t_ref[:half].reshape(half * na, v)
    high = t_ref[half:].reshape(half * na, v)
    dims = (((1,), (1,)), ((), ()))
    both = lax.dot_general(low, jnp.concatenate([pick, none], 0), dims, preferred_element_type=F32)
    both += lax.dot_general(high, jnp.concatenate([none, pick], 0), dims, preferred_element_type=F32)
    row_ref[0] = both.astype(BF).reshape(half, na, 2 * CAP)


def prepare_kernel(
    occ_ref, labels_ref, pos_ref, bits_ref, pick_own_ref, pick_other_ref, half_ref, spread_ref, expand_ref
):
    na, v = bits_ref.shape
    labels = labels_ref[...].reshape(1, v)
    pos = pos_ref[...]
    tr = lax.axis_index("tr")
    place = lax.broadcasted_iota(jnp.int32, (na, v), 0) + lax.axis_index("su") * na
    here = lax.broadcasted_iota(jnp.int32, (na, v), 1) == place
    labels_a = jnp.sum(jnp.where(here, labels, 0).astype(F32), axis=1, keepdims=True).astype(jnp.int32)
    plane = jnp.bitwise_xor(jnp.bitwise_xor(labels_a, labels), occ_ref[tr])
    bits = jnp.zeros((na, v), jnp.int32)
    for i in range(IW):
        bits += jnp.where(plane == occ_ref[i], 1 << i, 0)
    bits_ref[...] = bits
    rows_a = jnp.broadcast_to(labels_a, pick_own_ref.shape[1:])
    for i in range(IW):
        for ref, j in ((pick_own_ref, tr), (pick_other_ref, jnp.bitwise_xor(tr, 1))):
            ref[i] = jnp.right_shift(jnp.bitwise_xor(rows_a, jnp.bitwise_xor(occ_ref[i], occ_ref[j])), 1)
    upper = lax.broadcasted_iota(jnp.int32, rows_a.shape, 1) // CAP
    for i in range(IW):
        irrep = jnp.bitwise_xor(rows_a, jnp.bitwise_xor(occ_ref[i], occ_ref[tr]))
        half_ref[i] = (jnp.bitwise_and(irrep, 1) == upper).astype(jnp.int32)
    wide = lax.broadcasted_iota(jnp.int32, spread_ref.shape, 0) == labels * CAP + pos
    spread_ref[...] = wide.astype(F32).astype(BF)
    pair = lax.broadcasted_iota(jnp.int32, expand_ref.shape, 0) == jnp.bitwise_and(labels, 1) * CAP + pos
    expand_ref[...] = pair.astype(F32).astype(BF)


SMEM = pl.BlockSpec(memory_space=pltpu.SMEM)
VMEM = pl.BlockSpec(memory_space=pltpu.VMEM)
ANY = pl.BlockSpec(memory_space=pl.ANY)


def windowed(kernel, window):
    if window is None:
        return functools.partial(kernel, None), [], []
    return kernel, [SMEM], [window]


def pack_give(window, labels, t, w):
    nk, v, _ = w.shape
    kernel, specs, args = windowed(give_kernel, window)
    return pl.pallas_call(
        kernel,
        out_shape=(
            jax.ShapeDtypeStruct((1, nk // 2, CAP, v), BF),
            jax.ShapeDtypeStruct((1, v), jnp.int32),
            jax.ShapeDtypeStruct((1, 128), jnp.int32),
            jax.ShapeDtypeStruct(t.shape, BF),
            jax.ShapeDtypeStruct((nk // 2, v, v), BF),
        ),
        in_specs=specs + [ANY] * 3,
        out_specs=(VMEM,) * 5,
        scratch_shapes=[
            pltpu.VMEM((v,), jnp.int32),
            pltpu.VMEM((nk // 2, v, v), BF),
            pltpu.SemaphoreType.DMA((nk + 2,)),
        ],
        compiler_params=pltpu.CompilerParams(vmem_limit_bytes=8 * 2**20),
        name="pack_give",
    )(*args, labels, t, w)


def pack_keep(window, pos, t, w):
    nk, v, _ = w.shape
    ni, na, _ = t.shape
    kernel, specs, args = windowed(keep_kernel, window)
    return pl.pallas_call(
        kernel,
        out_shape=(
            jax.ShapeDtypeStruct((1, ni // 2, na, 2 * CAP), BF),
            jax.ShapeDtypeStruct((1, nk, CAP, v), BF),
        ),
        in_specs=specs + [VMEM] * 3,
        out_specs=(VMEM, VMEM),
        compiler_params=pltpu.CompilerParams(vmem_limit_bytes=8 * 2**20),
        cost_estimate=pl.CostEstimate(flops=0, bytes_accessed=4 * 2**20, transcendentals=0),
        name="pack_keep",
    )(*args, pos, t, w)


def prepare(occupied, labels, pos, na):
    v = labels.shape[0]
    pick = jax.ShapeDtypeStruct((IW, na, 2 * CAP), jnp.int32)
    return pl.pallas_call(
        prepare_kernel,
        out_shape=(
            jax.ShapeDtypeStruct((na, v), jnp.int32),
            pick,
            pick,
            pick,
            jax.ShapeDtypeStruct((8 * CAP, v), BF),
            jax.ShapeDtypeStruct((2 * CAP, v), BF),
        ),
        in_specs=[SMEM, VMEM, VMEM],
        out_specs=(VMEM,) * 6,
        compiler_params=pltpu.CompilerParams(vmem_limit_bytes=8 * 2**20),
        name="prepare",
    )(occupied, labels, pos)


OFFSETS = (0, 1, -1, 2, -2, 3, -3, 4)


def join_kernel(*refs):
    out_ref = refs[-1]
    at = 0
    for ref in refs[:-1]:
        out_ref[at : at + ref.shape[0]] = ref[...]
        at += ref.shape[0]


def join(name, *parts):
    shape = (sum(p.shape[0] for p in parts), *parts[0].shape[1:])
    size = 2 * 4 * math.prod(shape)
    return pl.pallas_call(
        join_kernel,
        out_shape=jax.ShapeDtypeStruct(shape, parts[0].dtype),
        in_specs=[VMEM] * len(parts),
        out_specs=VMEM,
        compiler_params=pltpu.CompilerParams(vmem_limit_bytes=8 * 2**20),
        cost_estimate=pl.CostEstimate(flops=0, bytes_accessed=size, transcendentals=0),
        name=name,
    )(*parts)


def lines(piece, first):
    return [lax.ppermute(piece, "tr", line(first, flip)) for flip in (1, 2, 3)]


def gather(keep, got, t, beside=lambda parts: ()):
    rows = lines(t, True)
    d = join("join_w", keep, got)
    a1 = lax.ppermute(d, "su", ODD_LINKS)
    b1 = lax.ppermute(d, "su", EVEN_LINKS)
    row = join("join_row", t, *rows)
    planes = lines(row, False)
    a2 = lax.ppermute(b1, "su", ODD_LINKS)
    b2 = lax.ppermute(a1, "su", EVEN_LINKS)
    a3 = lax.ppermute(b2, "su", ODD_LINKS)
    b3 = lax.ppermute(a2, "su", EVEN_LINKS)
    extra, a3 = lax.optimization_barrier((beside([d, a1, b1, a2, b2]), a3))
    a4 = lax.ppermute(b3[:1], "su", ODD_LINKS)
    b4 = lax.ppermute(a3[1:], "su", EVEN_LINKS)
    return [row, *planes], [d, a1, b1, a2, b2, a3, b3], a4, b4, extra


def blocks(d_refs, j, d_cat):
    _, ne, cap, v = d_refs[0].shape
    wide = ne * cap
    for n, d_ref in enumerate(d_refs):
        d_cat[n * wide : (n + 1) * wide] = d_ref[j].reshape(wide, v)


def other_kernel(*refs):
    t_refs, d_refs, (other_ref, t_cat, rest_ref, t_all, d_cat, sems) = refs[:4], refs[4:-6], refs[-6:]
    copies = [pltpu.make_async_copy(t_ref, t_all.at[NX * n : NX * n + NX], sems.at[n]) for n, t_ref in enumerate(t_refs)]
    for copy in copies:
        copy.start()
    _, ne, cap, v = d_refs[0].shape
    half_i, na = t_all.shape[1:3]
    rows = half_i * na
    wide = ne * cap
    blocks(d_refs, 1, d_cat)
    tr = lax.axis_index("tr")
    z = lax.axis_index("su")
    x, y, core = tr // (2 * NY), (tr // 2) % NY, tr % 2
    way = 1 - 2 * (z % 2)
    for copy in copies:
        copy.wait()
    for n, off in enumerate(OFFSETS):
        block = (z - off * way + NZ) % NZ
        pair = []
        for e in range(ne):
            chip = block * ne + e
            dx = jnp.bitwise_xor(chip // NY, x)
            dy = jnp.bitwise_xor(chip % NY, y)
            at = jnp.where(core == 0, dy * NX + dx, dx * NY + dy)
            pair.append(t_all[at].reshape(rows, 2 * CAP))
        for h in range(2):
            lanes = slice(h * CAP, (h + 1) * CAP)
            both = jnp.concatenate([pair[0][:, lanes], pair[1][:, lanes]], 1)
            if n < len(d_refs):
                t_cat[h, :, n * wide : (n + 1) * wide] = both
            else:
                rest_ref[h] = both
    for h in range(2):
        other_ref[h] = jnp.dot(t_cat[h], d_cat[...], preferred_element_type=F32)


def other_part(t_parts, d_parts):
    chips, half_i, na, lanes = t_parts[0].shape
    _, ne, cap, v = d_parts[0].shape
    rows = half_i * na
    wide = ne * cap
    depth = len(d_parts) * wide
    return pl.pallas_call(
        other_kernel,
        out_shape=(
            jax.ShapeDtypeStruct((2, rows, v), F32),
            jax.ShapeDtypeStruct((2, rows, depth), BF),
            jax.ShapeDtypeStruct((2, rows, wide), BF),
        ),
        in_specs=[ANY] * len(t_parts) + [VMEM] * len(d_parts),
        out_specs=(VMEM, VMEM, VMEM),
        scratch_shapes=[
            pltpu.VMEM((len(t_parts) * chips, half_i, na, lanes), BF),
            pltpu.VMEM((depth, v), BF),
            pltpu.SemaphoreType.DMA((len(t_parts),)),
        ],
        compiler_params=pltpu.CompilerParams(vmem_limit_bytes=20 * 2**20),
        cost_estimate=pl.CostEstimate(flops=4 * rows * v * depth, bytes_accessed=6 * 2**20, transcendentals=0),
        name="other_part",
    )(*t_parts, *d_parts)


def own_kernel(t_cat, *refs):
    d_refs, (own_ref, d_cat) = refs[:-2], refs[-2:]
    blocks(d_refs, 0, d_cat)
    for h in range(2):
        own_ref[h] = jnp.dot(t_cat[h], d_cat[...], preferred_element_type=F32)


def own_part(t_cat, d_parts):
    _, rows, depth = t_cat.shape
    v = d_parts[0].shape[3]
    return pl.pallas_call(
        own_kernel,
        out_shape=jax.ShapeDtypeStruct((2, rows, v), F32),
        in_specs=[VMEM] * (1 + len(d_parts)),
        out_specs=VMEM,
        scratch_shapes=[pltpu.VMEM((depth, v), BF)],
        compiler_params=pltpu.CompilerParams(vmem_limit_bytes=12 * 2**20),
        cost_estimate=pl.CostEstimate(flops=4 * rows * v * depth, bytes_accessed=4 * 2**20, transcendentals=0),
        name="own_part",
    )(t_cat, *d_parts)


def far_sum(h, sums_ref, rest_ref, d_ref):
    _, ne, cap, v = d_ref.shape
    return sums_ref[h] + jnp.dot(rest_ref[h], d_ref[0].reshape(ne * cap, v), preferred_element_type=F32)


def far_kernel(sums_ref, rest_ref, d_ref, out_ref):
    for h in range(2):
        out_ref[h] = far_sum(h, sums_ref, rest_ref, d_ref)


def far_part(sums, rest, d):
    return pl.pallas_call(
        far_kernel,
        out_shape=jax.ShapeDtypeStruct(sums.shape, F32),
        in_specs=[VMEM] * 3,
        out_specs=VMEM,
        compiler_params=pltpu.CompilerParams(vmem_limit_bytes=8 * 2**20),
        name="far_part",
    )(sums, rest, d)


def spread_kernel(spread_ref, *refs):
    d_refs, (own_ref, other_ref, d_cat) = refs[:-3], refs[-3:]
    dims = (((1,), (1,)), ((), ()))
    for j, ref in enumerate((own_ref, other_ref)):
        blocks(d_refs, j, d_cat)
        wide = lax.dot_general(d_cat[...], spread_ref[...], dims, preferred_element_type=F32)
        ref[...] = wide.astype(BF).reshape(ref.shape)


def spread_blocks(spread, d_parts):
    _, ne, cap, v = d_parts[0].shape
    count = len(d_parts) * ne
    out = jax.ShapeDtypeStruct((count, cap, spread.shape[0]), BF)
    return pl.pallas_call(
        spread_kernel,
        out_shape=(out, out),
        in_specs=[VMEM] * (1 + len(d_parts)),
        out_specs=(VMEM, VMEM),
        scratch_shapes=[pltpu.VMEM((count * cap, v), BF)],
        compiler_params=pltpu.CompilerParams(vmem_limit_bytes=8 * 2**20),
        cost_estimate=pl.CostEstimate(
            flops=4 * count * cap * v * spread.shape[0], bytes_accessed=4 * 2**20, transcendentals=0
        ),
        name="spread",
    )(spread, *d_parts)


def put_block(d_early, d_late, first, second, d_cat, at):
    src = block_at(first, second)
    early, late = d_early.shape[0], d_late.shape[0]
    near = d_early[jnp.minimum(src, early - 1)]
    far = d_late[jnp.clip(src - early, 0, late - 1)]
    far = jnp.where(src < early + late, far, jnp.zeros_like(far))
    d_cat[at : at + CAP] = jnp.where(src < early, near, far)


def block_at(first, second):
    tr = lax.axis_index("tr")
    z = lax.axis_index("su")
    x, y, core = tr // (2 * NY), (tr // 2) % NY, tr % 2
    to_x = jnp.bitwise_xor(x, jnp.where(core == 0, first, second))
    to_y = jnp.bitwise_xor(y, jnp.where(core == 0, second, first))
    ahead = (z - (2 * to_x + to_y // 2)) * (1 - 2 * (z % 2))
    hops = (ahead + 2 * NZ) % NZ
    arrival = jnp.where(hops == 0, 0, jnp.where(hops <= NZ // 2, 2 * hops - 1, 2 * (NZ - hops)))
    return 2 * arrival + to_y % 2


def pair_lanes(one, two, h):
    lanes = slice(h * CAP, (h + 1) * CAP)
    return jnp.concatenate([one[:, lanes], two[:, lanes]], 1)


def flat(piece):
    return piece.reshape(piece.shape[0] * piece.shape[1], piece.shape[2])


def early_kernel(*refs):
    t_refs, (d_early, d_late, other_ref, t_cat, d_cat) = refs[:-5], refs[-5:]
    lanes = 2 * CAP
    for second, t_ref in enumerate(t_refs):
        for p in range(NX // 2):
            one, two = flat(t_ref[2 * p]), flat(t_ref[2 * p + 1])
            at = (second * (NX // 2) + p) * lanes
            for h in range(2):
                t_cat[h, :, at : at + lanes] = pair_lanes(one, two, h)
            for u in range(2):
                put_block(d_early, d_late, 2 * p + u, second, d_cat, at + u * CAP)
    left = t_cat[...].reshape(2 * t_cat.shape[1], t_cat.shape[2])
    other_ref[...] = jnp.dot(left, d_cat[...], preferred_element_type=F32).reshape(other_ref.shape)


def early_sums(t_parts, d_other):
    chips, half_i, na, lanes = t_parts[0].shape
    rows = half_i * na
    depth = len(t_parts) * chips * CAP
    wide = d_other[0].shape[2]
    return pl.pallas_call(
        early_kernel,
        out_shape=(jax.ShapeDtypeStruct((2, rows, wide), F32), jax.ShapeDtypeStruct((2, rows, depth), BF)),
        in_specs=[VMEM] * (len(t_parts) + 2),
        out_specs=(VMEM, VMEM),
        scratch_shapes=[pltpu.VMEM((depth, wide), BF)],
        compiler_params=pltpu.CompilerParams(vmem_limit_bytes=16 * 2**20),
        cost_estimate=pl.CostEstimate(flops=4 * rows * wide * depth, bytes_accessed=6 * 2**20, transcendentals=0),
        name="early_sums",
    )(*t_parts, *d_other)


def keep_pair(sums, pick):
    lanes = 2 * CAP
    out = sums[:, :lanes]
    for g in range(1, 4):
        out = jnp.where(pick == g, sums[:, g * lanes : (g + 1) * lanes], out)
    return out


def other_pair_kernel(pick_ref, *refs):
    t_refs, (sums_ref, d_early, d_late, other_ref, late_ref, rest_ref, d_cat) = refs[:NX], refs[NX:]
    last = t_refs[-1]
    lanes = 2 * CAP
    for p in range(NX // 2):
        one, two = flat(last[2 * p]), flat(last[2 * p + 1])
        for h in range(2):
            late_ref[h, :, p * lanes : (p + 1) * lanes] = pair_lanes(one, two, h)
    for first in range(NX):
        put_block(d_early, d_late, first, NX - 1, d_cat, first * CAP)
    ni, na = other_ref.shape[:2]
    half_i = ni // 2
    for h in range(2):
        sums = sums_ref[h] + jnp.dot(late_ref[h], d_cat[...], preferred_element_type=F32)
        for u in range(half_i):
            i = h * half_i + u
            other_ref[i] = keep_pair(sums[u * na : (u + 1) * na], pick_ref[i])
    tr = lax.axis_index("tr")
    far = (lax.axis_index("su") + NZ // 2) % NZ
    x, y, core = tr // (2 * NY), (tr // 2) % NY, tr % 2
    pair = []
    for e in range(2):
        dx = jnp.bitwise_xor(far // 2, x)
        dy = jnp.bitwise_xor(2 * (far % 2) + e, y)
        first = jnp.where(core == 0, dx, dy)
        second = jnp.where(core == 0, dy, dx)
        piece = t_refs[0][first]
        for n in range(1, NX):
            piece = jnp.where(second == n, t_refs[n][first], piece)
        pair.append(flat(piece))
    for h in range(2):
        rest_ref[h] = pair_lanes(*pair, h)


def other_pair(pick, t_parts, sums, d):
    chips, half_i, na, lanes = t_parts[0].shape
    rows = half_i * na
    return pl.pallas_call(
        other_pair_kernel,
        out_shape=(
            jax.ShapeDtypeStruct(pick.shape, F32),
            jax.ShapeDtypeStruct((2, rows, chips * CAP), BF),
            jax.ShapeDtypeStruct((2, rows, lanes), BF),
        ),
        in_specs=[VMEM] * (4 + len(t_parts)),
        out_specs=(VMEM, VMEM, VMEM),
        scratch_shapes=[pltpu.VMEM((chips * CAP, sums.shape[2]), BF)],
        compiler_params=pltpu.CompilerParams(vmem_limit_bytes=12 * 2**20),
        cost_estimate=pl.CostEstimate(
            flops=4 * rows * sums.shape[2] * chips * CAP, bytes_accessed=6 * 2**20, transcendentals=0
        ),
        name="other_pair",
    )(pick, *t_parts, sums, *d)


def spread_far(d_ref, spread_ref):
    _, ne, cap, v = d_ref.shape
    dims = (((1,), (1,)), ((), ()))
    wide = lax.dot_general(d_ref[0].reshape(ne * cap, v), spread_ref[...], dims, preferred_element_type=F32)
    return wide.astype(BF)


def far_pair_kernel(pick_ref, spread_ref, sums_ref, rest_ref, d_ref, out_ref):
    right = spread_far(d_ref, spread_ref)
    ni, na = out_ref.shape[:2]
    left = rest_ref[...].reshape(ni * na, rest_ref.shape[2])
    sums = jnp.dot(left, right, preferred_element_type=F32)
    for i in range(ni):
        out_ref[i] = sums_ref[i] + keep_pair(sums[i * na : (i + 1) * na], pick_ref[i])


def far_pair(pick, spread, sums, rest, d):
    return pl.pallas_call(
        far_pair_kernel,
        out_shape=jax.ShapeDtypeStruct(pick.shape, F32),
        in_specs=[VMEM] * 5,
        out_specs=VMEM,
        compiler_params=pltpu.CompilerParams(vmem_limit_bytes=8 * 2**20),
        name="far_pair",
    )(pick, spread, sums, rest, d)


def own_pair_kernel(
    pick_ref, spread_ref, t_cat, late_ref, d_early, d_late, rest_ref, far_ref, own_ref, left_cat, d_cat
):
    at = 0
    for ref in (t_cat, late_ref, rest_ref):
        left_cat[:, :, at : at + ref.shape[2]] = ref[...]
        at += ref.shape[2]
    for second in range(NX):
        for first in range(NX):
            put_block(d_early, d_late, first, second, d_cat, (second * NX + first) * CAP)
    d_cat[NX * NX * CAP :] = spread_far(far_ref, spread_ref)
    ni, na = own_ref.shape[:2]
    left = left_cat[...].reshape(ni * na, left_cat.shape[2])
    sums = jnp.dot(left, d_cat[...], preferred_element_type=F32)
    for i in range(ni):
        own_ref[i] = keep_pair(sums[i * na : (i + 1) * na], pick_ref[i])


def own_pair(pick, spread, t_cat, late, d, rest, far):
    rows = late.shape[1]
    depth = t_cat.shape[2] + late.shape[2] + rest.shape[2]
    wide = d[0].shape[2]
    return pl.pallas_call(
        own_pair_kernel,
        out_shape=jax.ShapeDtypeStruct(pick.shape, F32),
        in_specs=[VMEM] * 8,
        out_specs=VMEM,
        scratch_shapes=[pltpu.VMEM((2, rows, depth), BF), pltpu.VMEM((depth, wide), BF)],
        compiler_params=pltpu.CompilerParams(vmem_limit_bytes=12 * 2**20),
        cost_estimate=pl.CostEstimate(flops=4 * rows * wide * depth, bytes_accessed=4 * 2**20, transcendentals=0),
        name="own_pair",
    )(pick, spread, t_cat, late, *d, rest, far)


def last_kernel(width_ref, bits_ref, half_ref, expand_ref, own_ref, got_ref, out_ref, fits_ref):
    fits_ref[0] = (width_ref[0, 0] <= CAP).astype(jnp.int32)
    ni, na, lanes = own_ref.shape
    sums = jnp.where(half_ref[...] != 0, own_ref[...] + got_ref[...], 0.0)
    sums = sums.astype(BF).reshape(ni * na, lanes)
    wide = jnp.dot(sums, expand_ref[...], preferred_element_type=F32)
    for i in range(ni):
        keep = jnp.bitwise_and(bits_ref[...], 1 << i) != 0
        out_ref[i] = jnp.where(keep, wide[i * na : (i + 1) * na], 0.0).astype(BF)


def window_kernel(before_ref, own_ref, got_ref, rest_ref, d_ref, out_ref):
    for h in range(2):
        out_ref[h] = before_ref[h] + far_sum(h, own_ref, rest_ref, d_ref) + got_ref[h]


def body(amplitudes, integrals, occupied_irreps, virtual_irreps):
    ni, _, na, v = amplitudes.shape
    t = amplitudes.reshape(ni, na, v)
    w = integrals.reshape(integrals.shape[0], v, v)

    def pack(window):
        give, pos, width, t_here, w_here = pack_give(window, virtual_irreps, t, w)
        got = lax.ppermute(give, "tr", SWAP)
        row, keep = pack_keep(window, pos, t_here, w_here)
        return keep, got, row, pos, width

    keep, got, row, pos, width = pack(None)
    bits, pick_own, pick_other, half, spread, expand = prepare(occupied_irreps, virtual_irreps, pos, na)
    t_parts, d_parts, a4, b4, d_two = gather(keep, got, row, functools.partial(spread_blocks, spread))
    d_three = spread_blocks(spread, d_parts[5:])
    d_own, d_other = zip(d_two, d_three)
    sums_other, t_cat = early_sums(t_parts[:-1], d_other)
    other, t_late, rest = other_pair(pick_other, t_parts, sums_other, d_other)
    other, a4, b4 = lax.optimization_barrier((other, a4, b4))
    got = lax.ppermute(far_pair(pick_other, spread, other, rest, b4), "tr", SWAP)
    own = own_pair(pick_own, spread, t_cat, t_late, d_own, rest, a4)
    fast, fits = pl.pallas_call(
        last_kernel,
        out_shape=(jax.ShapeDtypeStruct((ni, na, v), BF), jax.ShapeDtypeStruct((1,), jnp.int32)),
        in_specs=[VMEM] * 6,
        out_specs=(VMEM, SMEM),
        compiler_params=pltpu.CompilerParams(vmem_limit_bytes=8 * 2**20),
        name="last_part",
    )(width, bits, half, expand, own, got)

    def all_windows():
        def window(n, before):
            keep, got, row, _, _ = pack(jnp.full((1,), n, jnp.int32))
            t_parts, d_parts, a4, b4, _ = gather(keep, got, row)
            other, t_cat, rest = other_part(t_parts, d_parts)
            got = lax.ppermute(far_part(other, rest, b4), "tr", SWAP)
            parts = (own_part(t_cat, d_parts), got, rest, a4)
            return pl.pallas_call(
                window_kernel,
                out_shape=jax.ShapeDtypeStruct(before.shape, F32),
                in_specs=[VMEM] * (1 + len(parts)),
                out_specs=VMEM,
                compiler_params=pltpu.CompilerParams(vmem_limit_bytes=16 * 2**20),
                name="window_part",
            )(before, *parts)

        windows = (width[0, 0] + CAP - 1) // CAP
        sums = lax.fori_loop(0, windows, window, jnp.zeros((2, ni // 2 * na, v), F32))
        label_j = occupied_irreps[lax.axis_index("tr")]
        labels_a = lax.dynamic_slice_in_dim(virtual_irreps, lax.axis_index("su") * na, na, 0)
        parity = jnp.bitwise_xor(occupied_irreps[:ni, None, None], label_j)
        parity = jnp.bitwise_xor(parity, labels_a[None, :, None])
        keep = jnp.bitwise_xor(parity, virtual_irreps[None, None, :]) == 0
        return jnp.where(keep, sums.reshape(ni, na, v).astype(BF), jnp.zeros((), BF))

    out = lax.cond(fits[0] == 1, lambda: fast, all_windows)
    return out.reshape(ni, 1, na, v)


def solution(mesh):
    return jax.shard_map(
        body,
        mesh=mesh,
        in_specs=(P(None, "tr", "su", None), P("su", None, "tr", None), P(), P()),
        out_specs=P(None, "tr", "su", None),
        check_vma=False,
    )
```
